128 devices in a mesh: region: 4 (over z_hi, core), tile: 32 (over x, y, z_lo).
Axes of the slice: x: 4, y: 4, z: 4 (z_hi: 2, z_lo: 2; z = z_hi * 2 + z_lo), core: 2. Of those that a mesh axis runs over, the one named last changes fastest.
Arguments:
- tokens: bfloat16 [512, 512, 512], P('tile', 'region'), may hold values from -6 to 6
- pore_mask: int32 [512, 512], P('tile', 'region'), may hold values 0 or 1
- solid_embed: float32 [512], replicated, may hold values from -4 to 4
- fine_query: bfloat16 [512, 512], replicated, as said below
- fine_key: bfloat16 [512, 512], replicated, as said below
- fine_value: bfloat16 [512, 512], replicated, may hold values from -0.25 to 0.25
- fine_out: bfloat16 [512, 512], replicated, may hold values from -0.25 to 0.25
- fine_scale: float32 [8], replicated, may hold values from 1 to 16
- coarse_query: bfloat16 [512, 512], replicated, as said below
- coarse_key: bfloat16 [512, 512], replicated, as said below
- coarse_value: bfloat16 [512, 512], replicated, may hold values from -0.25 to 0.25
- coarse_out: bfloat16 [512, 512], replicated, may hold values from -0.25 to 0.25
- coarse_scale: float32 [8], replicated, may hold values from 1 to 16
- mlp_in: bfloat16 [512, 2048], replicated, may hold values from -0.25 to 0.25
- mlp_out: bfloat16 [2048, 512], replicated, may hold values from -0.125 to 0.125
Outputs:
- updated: bfloat16 [512, 512, 512], P('tile', 'region')
The draws below stay inside these ranges and needn't reach their ends.
Inputs may be any that keep to these rules, and one draw needn't show every extreme that they name: `fine_query`: entries of a projection of fan-in 512. `fine_key`: entries of a projection of fan-in 512. `coarse_query`: entries of a projection of fan-in 512. `coarse_key`: entries of a projection of fan-in 512.
All inputs are finite; a program needn't handle non-finite values. No bound on the sum of `pore_mask` on one device may be relied on, other than what follows from the above.
Results may differ from the reference program's by a relative error of at most 0.0081.
Values may be sent and summed in bfloat16 or wider, within the bound.
A program may use at most 128 MiB of HBM per device.

```python
import math
import jax
import jax.numpy as jnp
from jax import lax

D = 512
HEADS = 8
HEAD_DIM = 64
FF = 2048
RADIUS = 7
POOL = 8
TR = 16
ROWS = 512
COLS = 512
N_TILE = 32


def shared_projection(key, salt):
    noise = jax.random.normal(jax.random.fold_in(key, salt), (D, D), jnp.float32)
    return jnp.clip(noise, -6.0, 6.0) * D ** (-0.5)


def own_projection(key):
    noise = jax.random.normal(key, (D, D), jnp.float32)
    return jnp.clip(noise, -6.0, 6.0) * D ** (-0.5)


def draw_fine_query(key, part):
    common = shared_projection(key, 11)
    return common.astype(jnp.bfloat16)


def draw_fine_key(key, part):
    key = jax.random.fold_in(key, 2)
    own = own_projection(key)
    return own.astype(jnp.bfloat16)


def draw_coarse_query(key, part):
    common = shared_projection(key, 13)
    return common.astype(jnp.bfloat16)


def draw_coarse_key(key, part):
    key = jax.random.fold_in(key, 4)
    own = own_projection(key)
    return own.astype(jnp.bfloat16)


def with_ends(entries, key, smallest, high):
    longest = entries.shape.index(max(entries.shape))
    spots = []
    for shift in (0, 1):
        where = [jax.random.randint(jax.random.fold_in(key, axis), (), 0, length) for axis, length in enumerate(entries.shape)]
        where[longest] = (where[longest] + shift) % entries.shape[longest]
        spots.append(tuple(where))
    return entries.at[spots[0]].set(smallest).at[spots[1]].set(high)


def shard_levels(rng, shape, pieces, smallest, high):
    loudness = 1.0
    for dim, blocks in pieces:
        draws = jax.random.uniform(jax.random.fold_in(jax.random.fold_in(rng, 6), dim), (blocks,), jnp.float32, smallest / len(pieces), high / len(pieces))
        loudness = loudness * jnp.repeat(jnp.exp(draws), shape[dim] // blocks).reshape((-1,) + (1,) * (len(shape) - 1 - dim))
    return loudness


def bell_draw(key, shape, width, bound, shards=(), kind=jnp.bfloat16):
    values = jax.random.normal(key, shape, jnp.float32) * width
    if len(shards) > 0:
        values = shard_levels(key, shape, shards, -0.22, 0.18) * values
    return jnp.clip(values, min=-bound, max=bound).astype(kind)


def setup_inputs(seed: int = 0) -> dict:
    key_of = jax.random.split(jax.random.key(seed), 16)
    tokens = bell_draw(key_of[0], (ROWS, COLS, D), 1.0, 6.0, ((0, 32), (1, 4)))
    pore_mask = with_ends((jax.random.randint(key_of[1], (ROWS, COLS), 0, 3) < 1).astype(jnp.int32), jax.random.fold_in(key_of[1], 1), 0, 1)
    solid_embed = bell_draw(key_of[2], (D,), 1.0, 4.0, (), jnp.float32)
    fine_query = draw_fine_query(jax.random.fold_in(key_of[15], 71), 0)
    fine_key = draw_fine_key(jax.random.fold_in(key_of[15], 71), 0)
    fine_value = bell_draw(key_of[5], (D, D), D ** -0.5, 0.25)
    fine_out = bell_draw(key_of[6], (D, D), D ** -0.5, 0.25)
    fine_scale = jnp.clip(jnp.exp(jax.random.uniform(key_of[7], (HEADS,), jnp.float32, math.log(1.0), math.log(16.0))), 1.0, 16.0)
    coarse_query = draw_coarse_query(jax.random.fold_in(key_of[15], 71), 0)
    coarse_key = draw_coarse_key(jax.random.fold_in(key_of[15], 71), 0)
    coarse_value = bell_draw(key_of[10], (D, D), D ** -0.5, 0.25)
    coarse_out = bell_draw(key_of[11], (D, D), D ** -0.5, 0.25)
    coarse_scale = jnp.clip(jnp.exp(jax.random.uniform(key_of[12], (HEADS,), jnp.float32, math.log(1.0), math.log(16.0))), 1.0, 16.0)
    mlp_in = bell_draw(key_of[13], (D, FF), D ** -0.5, 0.25)
    mlp_out = bell_draw(key_of[14], (FF, D), FF ** -0.5, 0.125)
    return dict(tokens=tokens, pore_mask=pore_mask, solid_embed=solid_embed, fine_query=fine_query, fine_key=fine_key, fine_value=fine_value, fine_out=fine_out, fine_scale=fine_scale, coarse_query=coarse_query, coarse_key=coarse_key, coarse_value=coarse_value, coarse_out=coarse_out, coarse_scale=coarse_scale, mlp_in=mlp_in, mlp_out=mlp_out)


epsilon = 1e-06

def normalize_rows(values):
    return values * lax.rsqrt(lax.optimization_barrier(jnp.mean(values * values, axis=-1, keepdims=True)) + epsilon)

def head_normalize(projected):
    shape_in = projected.shape
    split = projected.reshape(shape_in[:-1] + (HEADS, HEAD_DIM))
    return normalize_rows(split).reshape(shape_in).astype(jnp.bfloat16)

def reference(tokens, pore_mask, solid_embed, fine_query, fine_key, fine_value, fine_out, fine_scale, coarse_query, coarse_key, coarse_value, coarse_out, coarse_scale, mlp_in, mlp_out):
    stream = tokens.astype(jnp.float32) + pore_mask.astype(jnp.float32)[..., None] * solid_embed
    normed = normalize_rows(stream).astype(jnp.bfloat16)
    flat_rows = normed.reshape(-1, D)
    head_shape = (ROWS, COLS, HEADS, HEAD_DIM)
    queries = head_normalize(jnp.dot(flat_rows, fine_query, preferred_element_type=jnp.float32)).reshape(head_shape)
    keys_all = head_normalize(jnp.dot(flat_rows, fine_key, preferred_element_type=jnp.float32)).reshape(head_shape)
    values_all = jnp.dot(flat_rows, fine_value, preferred_element_type=jnp.float32).astype(jnp.bfloat16).reshape(head_shape)
    margins = ((RADIUS, RADIUS), (RADIUS, RADIUS), (0, 0), (0, 0))
    padded_keys = jnp.pad(keys_all, margins, mode='wrap')
    padded_values = jnp.pad(values_all, margins, mode='wrap')
    fine_factor = fine_scale / math.sqrt(HEAD_DIM)
    span = 2 * RADIUS + 1
    offsets = jnp.arange(span * span, dtype=jnp.int32)

    def strip(strip_index):
        first_row = (strip_index * TR).astype(jnp.int32)
        query_rows = lax.dynamic_slice_in_dim(queries, first_row, TR, 0).astype(jnp.float32)

        def window_of(source, offset):
            shift_row = (offset // span).astype(jnp.int32)
            shift_col = (offset % span).astype(jnp.int32)
            zero = jnp.zeros((), jnp.int32)
            return lax.dynamic_slice(source, (first_row + shift_row, shift_col, zero, zero), (TR, COLS, HEADS, HEAD_DIM))

        def score(offset):
            return lax.optimization_barrier(jnp.sum(query_rows * window_of(padded_keys, offset).astype(jnp.float32), axis=-1)) * fine_factor

        def first_pass(state_now, offset):
            run_max, run_sum = state_now
            scores = score(offset)
            new_max = jnp.maximum(run_max, scores)
            run_sum = run_sum * jnp.exp(run_max - new_max) + jnp.exp(scores - new_max)
            return ((new_max, run_sum), None)
        start_state = (jnp.full((TR, COLS, HEADS), -jnp.inf, jnp.float32), jnp.zeros((TR, COLS, HEADS), jnp.float32))
        (row_max, row_sum), _ = lax.scan(first_pass, start_state, offsets)

        def second_pass(summed, offset):
            weights = (jnp.exp(score(offset) - row_max) / row_sum).astype(jnp.bfloat16)
            window_values = window_of(padded_values, offset)
            return (summed + weights.astype(jnp.float32)[..., None] * window_values.astype(jnp.float32), None)
        summed, _ = lax.scan(second_pass, jnp.zeros((TR, COLS, HEADS, HEAD_DIM), jnp.float32), offsets)
        return summed.astype(jnp.bfloat16)
    fine_attn = lax.map(strip, jnp.arange(N_TILE, dtype=jnp.int32)).reshape(ROWS * COLS, D)
    pooled = lax.optimization_barrier(jnp.mean(normed.reshape(ROWS // POOL, POOL, COLS // POOL, POOL, D), axis=(1, 3), dtype=jnp.float32))
    coarse_in = normalize_rows(pooled).astype(jnp.bfloat16).reshape(-1, D)
    coarse_heads = (-1, HEADS, HEAD_DIM)
    coarse_q = head_normalize(jnp.dot(coarse_in, coarse_query, preferred_element_type=jnp.float32)).reshape(coarse_heads)
    coarse_k = head_normalize(jnp.dot(coarse_in, coarse_key, preferred_element_type=jnp.float32)).reshape(coarse_heads)
    coarse_v = jnp.dot(coarse_in, coarse_value, preferred_element_type=jnp.float32).astype(jnp.bfloat16).reshape(coarse_heads)
    coarse_factor = (coarse_scale / math.sqrt(HEAD_DIM))[:, None, None]
    coarse_scores = jnp.einsum('qhd,khd->hqk', coarse_q.astype(jnp.float32), coarse_k.astype(jnp.float32), precision=lax.Precision.HIGHEST) * coarse_factor
    coarse_weights = jax.nn.softmax(coarse_scores, axis=-1)
    coarse_attn = jnp.einsum('hqk,khd->qhd', coarse_weights, coarse_v.astype(jnp.float32), precision=lax.Precision.HIGHEST)
    coarse_attn = coarse_attn.reshape(-1, D).astype(jnp.bfloat16)
    block_shape = (ROWS // POOL, POOL, COLS // POOL, POOL, D)
    feedback = jnp.dot(coarse_attn, coarse_out, preferred_element_type=jnp.float32).reshape(ROWS // POOL, 1, COLS // POOL, 1, D)
    fine_proj = jnp.dot(fine_attn, fine_out, preferred_element_type=jnp.float32).reshape(block_shape)
    mixed = (stream.reshape(block_shape) + fine_proj + feedback).reshape(-1, D)
    normed_mixed = normalize_rows(mixed).astype(jnp.bfloat16)
    hidden = jax.nn.gelu(jnp.dot(normed_mixed, mlp_in, preferred_element_type=jnp.float32), approximate=False).astype(jnp.bfloat16)
    updated = mixed + jnp.dot(hidden, mlp_out, preferred_element_type=jnp.float32)
    return updated.astype(jnp.bfloat16).reshape(ROWS, COLS, D)
```

```python
import functools
import math

import jax
import jax.numpy as jnp
import numpy as np
from jax import lax
from jax.experimental import pallas as pl
from jax.experimental.pallas import tpu as pltpu
from jax.sharding import PartitionSpec as P

F32, BF16 = jnp.float32, jnp.bfloat16
MESH = pl.DeviceIdType.MESH
HEADS = 8
EPS = 1e-6
BIG = 131072.0
LOG2E = math.log2(math.e)
TAIL = (
    -1.0002404059668364,
    -1.1475987944049173,
    -0.46737700467532134,
    -0.04592394901048988,
    0.005166375711832039,
    -0.00025544077122896525,
)
NT = (((1,), (1,)), ((), ()))


def mm(a, b):
    return jnp.dot(a, b, preferred_element_type=F32)


def gelu(x):
    z = jnp.abs(x)
    p = TAIL[5] * z + TAIL[4]
    for c in TAIL[3::-1]:
        p = p * z + c
    return jnp.maximum(x, 0.0) - z * jnp.exp2(p)


def block_ones():
    i = np.arange(256) // 64
    return jnp.asarray((i[:, None] == i[None, :]).astype(np.float32) / 64.0, BF16)


def key_tables():
    t = np.zeros((4, 8, 32, 128), np.float32)
    q = np.arange(16)
    for chunk in range(4):
        for row in range(8):
            away = np.abs(q - (8 * (chunk - 1) + row))
            t[chunk, row, :, 0:16] = np.where(away <= 7, 0.0, -BIG)[None, :]
        for col in range(32):
            t[chunk, :, col, 16:32] = np.where(np.abs(q - (col - 8)) <= 7, 0.0, -BIG)[None, :]
    return jnp.asarray(t.reshape(4, 256, 128), BF16)


def query_table():
    t = np.zeros((16, 16, 128), np.float32)
    for i in range(16):
        t[i, :, i] = 1.0
        t[:, i, 16 + i] = 1.0
    return jnp.asarray(t.reshape(256, 128), BF16)


def head_norm(p, ones):
    sq = (p * p).astype(BF16)
    ms = jnp.concatenate([mm(sq[:, :256], ones), mm(sq[:, 256:], ones)], axis=1)
    return (p * lax.rsqrt(ms + EPS)).astype(BF16)


def normalize(x):
    return x * lax.rsqrt(jnp.mean(x * x, axis=-1, keepdims=True) + EPS)


def queries_of(q_s, qt_ref, j, p):
    q = q_s[:, pl.ds(pl.multiple_of(16 * j, 16), 16), 128 * p : 128 * p + 128].reshape(256, 128)
    low = lax.broadcasted_iota(jnp.int32, (256, 128), 1) < 64
    zero = jnp.zeros_like(q)
    qt = qt_ref[...]
    return [
        jnp.concatenate([jnp.where(low, q, zero), qt], axis=1),
        jnp.concatenate([jnp.where(low, zero, q), qt], axis=1),
    ]


def chunk_of(ref, row, j, p, extra):
    cols = pl.ds(pl.multiple_of(16 * j, 16), 32)
    x = ref[row : row + 8, cols, 128 * p : 128 * p + 128].reshape(256, 128)
    return jnp.concatenate([x, extra], axis=1)


def soft(s, c):
    top = jnp.max(s, axis=-1, keepdims=True)
    return jnp.exp2((s - top) * c).astype(BF16), top * c


def merge(first, second):
    low = lax.broadcasted_iota(jnp.int32, first.shape, 1) < 64
    return jnp.where(low, first, second)


def attend_own(j, p, q_s, k_s, v_s, qt_ref, kt_ref, c_ref, o_s, l_s, m_s):
    qa, qb = queries_of(q_s, qt_ref, j, p)
    ones = jnp.ones((256, 128), BF16)
    keys = jnp.concatenate([chunk_of(k_s, 8 * i, j, p, kt_ref[1 + i]) for i in range(2)], axis=0)
    vals = jnp.concatenate([chunk_of(v_s, 8 * i, j, p, ones) for i in range(2)], axis=0)
    s = lax.dot_general(jnp.concatenate([qa, qb], axis=0), keys, NT, preferred_element_type=F32)
    wa, ma = soft(s[:256], c_ref[2 * p])
    wb, mb = soft(s[256:], c_ref[2 * p + 1])
    o = mm(jnp.concatenate([wa, wb], axis=0), vals)
    o_s[j, p] = merge(o[:256, :128], o[256:, :128])
    l_s[j, p] = merge(o[:256, 128:], o[256:, 128:])
    m_s[j, p] = merge(jnp.broadcast_to(ma, (256, 128)), jnp.broadcast_to(mb, (256, 128)))


def attend_all(j, p, q_s, ku_s, kd_s, vu_s, vd_s, qt_ref, kt_ref, c_ref, o_s, l_s, m_s):
    qa, qb = queries_of(q_s, qt_ref, j, p)
    ones = jnp.ones((256, 128), BF16)
    done = []
    for k_s, v_s, table, part in ((ku_s, vu_s, 0, slice(0, 128)), (kd_s, vd_s, 3, slice(128, 256))):
        keys = chunk_of(k_s, 0, j, p, kt_ref[table])
        vals = chunk_of(v_s, 0, j, p, ones)
        q = jnp.concatenate([qa[part], qb[part]], axis=0)
        s = lax.dot_general(q, keys, NT, preferred_element_type=F32)
        wa, ma = soft(s[:128], c_ref[2 * p])
        wb, mb = soft(s[128:], c_ref[2 * p + 1])
        o = mm(jnp.concatenate([wa, wb], axis=0), vals)
        o2 = merge(o[:128, :128], o[128:, :128])
        l2 = merge(o[:128, 128:], o[128:, 128:])
        m2 = merge(jnp.broadcast_to(ma, (128, 128)), jnp.broadcast_to(mb, (128, 128)))
        o1, l1, m1 = o_s[j, p, part], l_s[j, p, part], m_s[j, p, part]
        top = jnp.maximum(m1, m2)
        a1, a2 = jnp.exp2(m1 - top), jnp.exp2(m2 - top)
        done.append(((o1 * a1 + o2 * a2) / (l1 * a1 + l2 * a2)).astype(BF16))
    return jnp.concatenate(done, axis=0)


def project(n, wk_ref, wv_ref, ones):
    return head_norm(mm(n, wk_ref[...]), ones), mm(n, wv_ref[...]).astype(BF16)


def project_own(i, buf, wq_ref, wk_ref, wv_ref, ones, q_s, k_s, v_s):
    wide = buf[i]
    q_s[i] = head_norm(mm(wide[16:144], wq_ref[...]), ones)
    n = wide.astype(F32)[8:152].astype(BF16)
    k_s[i], v_s[i] = project(n, wk_ref, wv_ref, ones)


def project_halo(k, buf, wk_ref, wv_ref, ones, k_s, v_s):
    n = buf[:, pl.ds(pl.multiple_of(32 * k, 32), 48), :].astype(F32)[:, 8:40].astype(BF16)
    keys, vals = project(n.reshape(256, 512), wk_ref, wv_ref, ones)
    cols = pl.ds(pl.multiple_of(32 * k, 32), 32)
    k_s[:, cols, :] = keys.reshape(8, 32, 512)
    v_s[:, cols, :] = vals.reshape(8, 32, 512)


def stream_of(tok, mask, emb):
    m = mask.astype(F32)
    return tok.astype(F32) + jnp.concatenate([m] * 4, axis=1) * emb


def finish(j, fine, tok_ref, mask_ref, emb_ref, fb_s, wo_ref, w1_ref, w2_ref, out_ref):
    at = pl.ds(pl.multiple_of(16 * j, 16), 16)
    stream = stream_of(tok_ref[:, at, :].reshape(256, 512), mask_ref[:, at, :].reshape(256, 128), emb_ref[...])
    fb = fb_s[:, pl.ds(2 * j, 2)].reshape(2, 1, 16, 512)
    fb = jnp.broadcast_to(fb, (2, 8, 16, 512)).reshape(256, 512)
    mixed = stream + mm(fine, wo_ref[...]) + fb
    nm = normalize(mixed).astype(BF16)
    acc = mixed
    for f in range(4):
        part = slice(512 * f, 512 * f + 512)
        h = gelu(mm(nm, w1_ref[:, part])).astype(BF16)
        acc = acc + mm(h, w2_ref[part, :])
    out_ref[:, at, :] = acc.astype(BF16).reshape(16, 16, 512)


LEFT, OWN, RIGHT = pl.ds(0, 16), pl.ds(16, 128), pl.ds(144, 16)
FIRST, LAST = pl.ds(16, 16), pl.ds(128, 16)
N_COPIES = 42


def layer(
    tok_ref, mask_ref, emb_ref, wq_ref, wk_ref, wv_ref, wo_ref, cwq_ref, cwk_ref, cwv_ref, cwo_ref,
    w1_ref, w2_ref, ones_ref, qt_ref, kt_ref, c_ref, cc_ref, out_ref,
    buf, up_buf, dn_buf, q_s, k_s, v_s, ku_s, vu_s, kd_s, vd_s, o_s, l_s, m_s,
    psum, cin_s, cq_s, x_s, ck_s, cv_s, qz_s, po_s, ps_s, rz_s, rs_s, fb_s, send_sem, recv_sem,
):
    t, r = lax.axis_index("tile"), lax.axis_index("region")
    prev, following = (t + 31) % 32, (t + 1) % 32
    left, right = (r + 3) % 4, (r + 1) % 4
    g, z_lo = t // 2, t % 2
    z_hi, core = r // 2, r % 2
    z = 2 * z_hi + z_lo
    ones = ones_ref[...]

    def plane(step):
        return {"tile": 2 * ((g + step) % 16) + z_lo, "region": r}

    def column(step):
        other = (z + step) % 4
        return {"tile": 2 * g + other % 2, "region": 2 * (other // 2) + core}

    def copy(src, dst, index, where):
        return pltpu.make_async_remote_copy(
            src_ref=src, dst_ref=dst, send_sem=send_sem.at[index], recv_sem=recv_sem.at[index],
            device_id=where, device_id_type=MESH,
        )

    to_left, to_right = {"tile": t, "region": left}, {"tile": t, "region": right}
    barrier = pltpu.get_barrier_semaphore()
    for where in [to_left, to_right] + [{"tile": a, "region": b} for a in (prev, following) for b in (left, r, right)]:
        pl.semaphore_signal(barrier, inc=1, device_id=where, device_id_type=MESH)

    @pl.loop(1, 16)
    def _(step):
        pl.semaphore_signal(barrier, inc=1, device_id=plane(step), device_id_type=MESH)

    for step in (1, 2, 3):
        pl.semaphore_signal(barrier, inc=1, device_id=column(step), device_id_type=MESH)

    psum[...] = jnp.zeros_like(psum)

    @pl.loop(0, 16)
    def _(i):
        n = normalize(stream_of(tok_ref[i], mask_ref[i], emb_ref[...])).astype(BF16)
        buf[i, OWN, :] = n
        psum[i // 8] += n.astype(F32)

    up_buf[0] = jnp.zeros((176, 512), BF16)
    dn_buf[7] = jnp.zeros((176, 512), BF16)

    pl.semaphore_wait(barrier, 26)

    top, bottom = pl.ds(0, 7), pl.ds(9, 7)
    up_rows, dn_rows = pl.ds(1, 7), pl.ds(0, 7)
    sides = [
        copy(buf.at[:, FIRST, :], buf.at[:, RIGHT, :], 0, to_left),
        copy(buf.at[:, LAST, :], buf.at[:, LEFT, :], 1, to_right),
    ]
    corners = [
        copy(buf.at[top, LAST, :], dn_buf.at[dn_rows, LEFT, :], 2, {"tile": prev, "region": right}),
        copy(buf.at[bottom, LAST, :], up_buf.at[up_rows, LEFT, :], 3, {"tile": following, "region": right}),
        copy(buf.at[top, FIRST, :], dn_buf.at[dn_rows, RIGHT, :], 4, {"tile": prev, "region": left}),
        copy(buf.at[bottom, FIRST, :], up_buf.at[up_rows, RIGHT, :], 5, {"tile": following, "region": left}),
    ]

    def row_piece(k):
        cols = pl.ds(pl.multiple_of(16 + 32 * k, 16), 32)
        return (
            copy(buf.at[top, cols, :], dn_buf.at[dn_rows, cols, :], 6 + k, {"tile": prev, "region": r}),
            copy(buf.at[bottom, cols, :], up_buf.at[up_rows, cols, :], 10 + k, {"tile": following, "region": r}),
        )

    for c in sides + corners:
        c.start()

    @pl.loop(0, 4)
    def _(k):
        for c in row_piece(k):
            c.start()

    cin = normalize(jnp.sum(psum[...].reshape(32, 8, 512), axis=1) * (1.0 / 64.0)).astype(BF16)
    cin_s[...] = cin
    x_s[core, g] = cin

    def gather(step):
        return copy(cin_s, x_s.at[core, g], 13 + step, plane(step))

    @pl.loop(1, 16)
    def _(step):
        gather(step).start()

    cq = head_norm(mm(cin, cwq_ref[...]), ones)
    cq_s[...] = cq
    qz_s[z] = cq
    asks = [copy(cq_s, qz_s.at[z], 28 + step, column(step)) for step in (1, 2, 3)]
    for c in asks:
        c.start()

    @pl.loop(0, 16)
    def _(i):
        q_s[i] = head_norm(mm(buf[i, OWN, :], wq_ref[...]), ones)

    for c in sides:
        c.wait_recv()

    @pl.loop(0, 16)
    def _(i):
        n = buf[i].astype(F32)[8:152].astype(BF16)
        k_s[i], v_s[i] = project(n, wk_ref, wv_ref, ones)

    @pl.loop(1, 16)
    def _(step):
        gather(step).wait_recv()

    sibling = copy(x_s.at[core], x_s.at[core], 32, {"tile": t, "region": 2 * z_hi + 1 - core})
    sibling.start()

    @pl.loop(0, 4)
    def _(j):
        for p in range(4):
            attend_own(j, p, q_s, k_s, v_s, qt_ref, kt_ref, c_ref, o_s, l_s, m_s)

    sibling.wait_recv()
    for c in asks:
        c.wait_recv()
    coarse_part(x_s, qz_s, cwk_ref, cwv_ref, cc_ref, ones, ck_s, cv_s, po_s, ps_s)
    replies = []
    for step in (1, 2, 3):
        rows = pl.ds(pl.multiple_of(32 * ((z + step) % 4), 32), 32)
        replies.append(copy(po_s.at[rows, :], rz_s.at[z], 32 + step, column(step)))
        replies.append(copy(ps_s.at[:, rows, :], rs_s.at[z], 35 + step, column(step)))
    for c in replies:
        c.start()
    mine = pl.ds(pl.multiple_of(32 * z, 32), 32)
    rz_s[z] = po_s[mine, :]
    rs_s[z] = ps_s[:, mine, :]

    @pl.loop(4, 8)
    def _(j):
        for p in range(4):
            attend_own(j, p, q_s, k_s, v_s, qt_ref, kt_ref, c_ref, o_s, l_s, m_s)

    for c in replies:
        c.wait_recv()
    feedback = mm(coarse_join(rz_s, rs_s), cwo_ref[...])
    fb_s[...] = jnp.broadcast_to(feedback.reshape(32, 1, 512), (32, 8, 512)).reshape(2, 16, 8, 512)

    def halo(k):
        project_halo(k, up_buf, wk_ref, wv_ref, ones, ku_s, vu_s)
        project_halo(k, dn_buf, wk_ref, wv_ref, ones, kd_s, vd_s)

    for c in corners[:2]:
        c.wait_recv()
    for c in row_piece(0):
        c.wait_recv()
    halo(0)

    @pl.loop(0, 8)
    def _(j):
        @pl.when(j % 2 == 1)
        def _():
            k = (j + 1) // 2

            @pl.when(j < 7)
            def _():
                for c in row_piece(k):
                    c.wait_recv()

            @pl.when(j == 7)
            def _():
                for c in corners[2:]:
                    c.wait_recv()

            halo(k)

        fine = jnp.concatenate(
            [
                attend_all(j, p, q_s, ku_s, kd_s, vu_s, vd_s, qt_ref, kt_ref, c_ref, o_s, l_s, m_s)
                for p in range(4)
            ],
            axis=1,
        )
        finish(j, fine, tok_ref, mask_ref, emb_ref, fb_s, wo_ref, w1_ref, w2_ref, out_ref)

    for c in sides + corners + asks + [sibling] + replies:
        c.wait_send()

    @pl.loop(0, 4)
    def _(k):
        for c in row_piece(k):
            c.wait_send()

    @pl.loop(1, 16)
    def _(step):
        gather(step).wait_send()


def coarse_part(x_s, qz_s, wk_ref, wv_ref, cc_ref, ones, ck_s, cv_s, po_s, ps_s):
    @pl.loop(0, 4)
    def _(i):
        x = x_s[i // 2, pl.ds(8 * (i % 2), 8)].reshape(256, 512)
        rows = pl.ds(pl.multiple_of(256 * i, 256), 256)
        k, v = project(x, wk_ref, wv_ref, ones)
        ck_s[rows, :] = k
        cv_s[rows, :] = v

    q = qz_s[...].reshape(128, 512)
    lane = lax.broadcasted_iota(jnp.int32, (128, 128), 1)
    head = lax.broadcasted_iota(jnp.int32, (128, 256), 1) // 64
    tops = jnp.zeros((128, 128), F32)
    sums = jnp.zeros((128, 128), F32)
    for half in range(2):
        lanes = slice(256 * half, 256 * half + 256)
        qh = q[:, lanes]
        rows = jnp.concatenate([jnp.where(head == h, qh, jnp.zeros_like(qh)) for h in range(4)], axis=0)
        s = lax.dot_general(rows, ck_s[:, lanes], NT, preferred_element_type=F32)
        weights = []
        for h in range(4):
            c = cc_ref[4 * half + h]
            part = s[128 * h : 128 * h + 128]
            top = jnp.max(part, axis=-1, keepdims=True)
            w = jnp.exp2((part - top) * c)
            tops = jnp.where(lane == 4 * half + h, top * c, tops)
            sums = jnp.where(lane == 4 * half + h, jnp.sum(w, axis=-1, keepdims=True), sums)
            weights.append(w.astype(BF16))
        o = mm(jnp.concatenate(weights, axis=0), cv_s[:, lanes])
        picked = o[:128]
        for h in range(1, 4):
            picked = jnp.where(head == h, o[128 * h : 128 * h + 128], picked)
        po_s[:, lanes] = picked
    ps_s[0] = tops
    ps_s[1] = sums


def coarse_join(rz_s, rs_s):
    top = jnp.maximum(jnp.maximum(rs_s[0, 0], rs_s[1, 0]), jnp.maximum(rs_s[2, 0], rs_s[3, 0]))
    scale = [jnp.exp2(rs_s[i, 0] - top) for i in range(4)]
    total = sum(scale[i] * rs_s[i, 1] for i in range(4))
    low = lax.broadcasted_iota(jnp.int32, (32, 128), 1) < 64
    joined = jnp.zeros((32, 512), F32)
    for i in range(4):
        a = scale[i] / total
        wide = [
            jnp.where(low, jnp.broadcast_to(a[:, 2 * p : 2 * p + 1], (32, 128)), jnp.broadcast_to(a[:, 2 * p + 1 : 2 * p + 2], (32, 128)))
            for p in range(4)
        ]
        joined = joined + jnp.concatenate(wide, axis=1) * rz_s[i]
    return joined.astype(BF16)


def body(
    tokens, pore_mask, solid_embed, fine_query, fine_key, fine_value, fine_out, fine_scale,
    coarse_query, coarse_key, coarse_value, coarse_out, coarse_scale, mlp_in, mlp_out,
):
    mask = jnp.broadcast_to(pore_mask.astype(BF16)[..., None], (16, 128, 128))
    factor = LOG2E / math.sqrt(64)
    vm = pl.BlockSpec(memory_space=pltpu.VMEM)
    sm = pl.BlockSpec(memory_space=pltpu.SMEM)
    V = pltpu.VMEM
    return pl.pallas_call(
        layer,
        out_shape=jax.ShapeDtypeStruct((16, 128, 512), BF16),
        in_specs=[vm] * 16 + [sm] * 2,
        out_specs=vm,
        scratch_shapes=[
            V((16, 160, 512), BF16),
            V((8, 176, 512), BF16),
            V((8, 176, 512), BF16),
            V((16, 128, 512), BF16),
            V((16, 144, 512), BF16),
            V((16, 144, 512), BF16),
            V((8, 160, 512), BF16),
            V((8, 160, 512), BF16),
            V((8, 160, 512), BF16),
            V((8, 160, 512), BF16),
            V((8, 4, 256, 128), F32),
            V((8, 4, 256, 128), F32),
            V((8, 4, 256, 128), F32),
            V((2, 128, 512), F32),
            V((32, 512), BF16),
            V((32, 512), BF16),
            V((2, 16, 32, 512), BF16),
            V((1024, 512), BF16),
            V((1024, 512), BF16),
            V((4, 32, 512), BF16),
            V((128, 512), F32),
            V((2, 128, 128), F32),
            V((4, 32, 512), F32),
            V((4, 2, 32, 128), F32),
            V((2, 16, 8, 512), F32),
            pltpu.SemaphoreType.DMA((N_COPIES,)),
            pltpu.SemaphoreType.DMA((N_COPIES,)),
        ],
        compiler_params=pltpu.CompilerParams(
            collective_id=0, has_side_effects=True, vmem_limit_bytes=62 * 2**20
        ),
    )(
        tokens, mask, solid_embed.reshape(1, 512), fine_query, fine_key, fine_value, fine_out,
        coarse_query, coarse_key, coarse_value, coarse_out, mlp_in, mlp_out,
        block_ones(), query_table(), key_tables(), fine_scale * factor, coarse_scale * factor,
    )


def solution(mesh):
    placed = (P("tile", "region", None), P("tile", "region")) + (P(),) * 13
    return jax.shard_map(
        body, mesh=mesh, in_specs=placed, out_specs=P("tile", "region", None), check_vma=False
    )
```

```python
import functools
import math

import jax
import jax.numpy as jnp
import numpy as np
from jax import lax
from jax.experimental import pallas as pl
from jax.experimental.pallas import tpu as pltpu
from jax.sharding import PartitionSpec as P

F32, BF16 = jnp.float32, jnp.bfloat16
MESH = pl.DeviceIdType.MESH
HEADS = 8
EPS = 1e-6
BIG = 131072.0
FACTOR = math.log2(math.e) / 8.0
TAIL = (
    -1.0002404059668364,
    -1.1475987944049173,
    -0.46737700467532134,
    -0.04592394901048988,
    0.005166375711832039,
    -0.00025544077122896525,
)
NT = (((1,), (1,)), ((), ()))


def mm(a, b):
    return jnp.dot(a, b, preferred_element_type=F32)


def gelu(x):
    z = jnp.abs(x)
    p = TAIL[5] * z + TAIL[4]
    for c in TAIL[3::-1]:
        p = p * z + c
    return jnp.maximum(x, 0.0) - z * jnp.exp2(p)


def block_ones():
    i = np.arange(256) // 64
    return jnp.asarray((i[:, None] == i[None, :]).astype(np.float32) / 64.0, BF16)


def key_tables():
    t = np.zeros((4, 8, 32, 128), np.float32)
    q = np.arange(16)
    for chunk in range(4):
        for row in range(8):
            away = np.abs(q - (8 * (chunk - 1) + row))
            t[chunk, row, :, 0:16] = np.where(away <= 7, 0.0, -BIG)[None, :]
        for col in range(32):
            t[chunk, :, col, 16:32] = np.where(np.abs(q - (col - 8)) <= 7, 0.0, -BIG)[None, :]
    return jnp.asarray(t.reshape(4, 256, 128), BF16)


def query_table():
    t = np.zeros((16, 16, 128), np.float32)
    for i in range(16):
        t[i, :, i] = 1.0
        t[:, i, 16 + i] = 1.0
    return jnp.asarray(t.reshape(256, 128), BF16)


def head_norm(p, ones):
    sq = (p * p).astype(BF16)
    ms = jnp.concatenate([mm(sq[:, :256], ones), mm(sq[:, 256:], ones)], axis=1)
    return (p * lax.rsqrt(ms + EPS)).astype(BF16)


def normalize(x):
    return x * lax.rsqrt(jnp.mean(x * x, axis=-1, keepdims=True) + EPS)


def queries_of(q_s, qt_ref, j, p):
    q = q_s[:, pl.ds(pl.multiple_of(16 * j, 16), 16), 128 * p : 128 * p + 128].reshape(256, 128)
    low = lax.broadcasted_iota(jnp.int32, (256, 128), 1) < 64
    zero = jnp.zeros_like(q)
    qt = qt_ref[...]
    return [
        jnp.concatenate([jnp.where(low, q, zero), qt], axis=1),
        jnp.concatenate([jnp.where(low, zero, q), qt], axis=1),
    ]


def chunk_of(ref, row, j, p, extra):
    cols = pl.ds(pl.multiple_of(16 * j, 16), 32)
    x = ref[row : row + 8, cols, 128 * p : 128 * p + 128].reshape(256, 128)
    return jnp.concatenate([x, extra], axis=1)


def soft(s, c):
    top = jnp.max(s, axis=-1, keepdims=True)
    return jnp.exp2((s - top) * c).astype(BF16), top * c


def merge(first, second):
    low = lax.broadcasted_iota(jnp.int32, first.shape, 1) < 64
    return jnp.where(low, first, second)


def attend_own(j, p, q_s, k_s, v_s, qt_ref, kt_ref, c_ref, o_s, l_s, m_s):
    qa, qb = queries_of(q_s, qt_ref, j, p)
    ones = jnp.ones((256, 128), BF16)
    keys = jnp.concatenate([chunk_of(k_s, 8 * i, j, p, kt_ref[1 + i]) for i in range(2)], axis=0)
    vals = jnp.concatenate([chunk_of(v_s, 8 * i, j, p, ones) for i in range(2)], axis=0)
    s = lax.dot_general(jnp.concatenate([qa, qb], axis=0), keys, NT, preferred_element_type=F32)
    wa, ma = soft(s[:256], c_ref[2 * p])
    wb, mb = soft(s[256:], c_ref[2 * p + 1])
    o = mm(jnp.concatenate([wa, wb], axis=0), vals)
    o_s[j, p] = merge(o[:256, :128], o[256:, :128])
    l_s[j, p] = merge(o[:256, 128:], o[256:, 128:])
    m_s[j, p] = merge(jnp.broadcast_to(ma, (256, 128)), jnp.broadcast_to(mb, (256, 128)))


def attend_all(j, p, q_s, ku_s, kd_s, vu_s, vd_s, qt_ref, kt_ref, c_ref, o_s, l_s, m_s):
    qa, qb = queries_of(q_s, qt_ref, j, p)
    ones = jnp.ones((256, 128), BF16)
    done = []
    for k_s, v_s, table, part in ((ku_s, vu_s, 0, slice(0, 128)), (kd_s, vd_s, 3, slice(128, 256))):
        keys = chunk_of(k_s, 0, j, p, kt_ref[table])
        vals = chunk_of(v_s, 0, j, p, ones)
        q = jnp.concatenate([qa[part], qb[part]], axis=0)
        s = lax.dot_general(q, keys, NT, preferred_element_type=F32)
        wa, ma = soft(s[:128], c_ref[2 * p])
        wb, mb = soft(s[128:], c_ref[2 * p + 1])
        o = mm(jnp.concatenate([wa, wb], axis=0), vals)
        o2 = merge(o[:128, :128], o[128:, :128])
        l2 = merge(o[:128, 128:], o[128:, 128:])
        m2 = merge(jnp.broadcast_to(ma, (128, 128)), jnp.broadcast_to(mb, (128, 128)))
        o1, l1, m1 = o_s[j, p, part], l_s[j, p, part], m_s[j, p, part]
        top = jnp.maximum(m1, m2)
        a1, a2 = jnp.exp2(m1 - top), jnp.exp2(m2 - top)
        done.append(((o1 * a1 + o2 * a2) / (l1 * a1 + l2 * a2)).astype(BF16))
    return jnp.concatenate(done, axis=0)


def project(n, wk, wv, ones):
    return head_norm(mm(n, wk), ones), mm(n, wv).astype(BF16)


def stream_of(tok, mask, emb):
    m = mask.astype(F32)
    return tok.astype(F32) + jnp.concatenate([m] * 4, axis=1) * emb


def finish(start, cols, fine_s, tok_s, mask_s, emb_ref, fb_s, wo, w1_s, w2_s, out_s):
    count = 16 * cols
    at = pl.ds(pl.multiple_of(start, 16), cols)
    stream = stream_of(tok_s[:, at, :].reshape(count, 512), mask_s[:, at, :].reshape(count, 128), emb_ref[...])
    fb = fb_s[:, pl.ds(start // 8, cols // 8)].reshape(2, 1, cols, 512)
    fb = jnp.broadcast_to(fb, (2, 8, cols, 512)).reshape(count, 512)
    mixed = stream + mm(fine_s[:, at, :].reshape(count, 512), wo) + fb
    nm = normalize(mixed).astype(BF16)
    acc = mixed
    for f in range(4):
        part = slice(512 * f, 512 * f + 512)
        h = gelu(mm(nm, w1_s[:, part])).astype(BF16)
        acc = acc + mm(h, w2_s[part, :])
    out_s[:, at, :] = acc.astype(BF16).reshape(16, cols, 512)


LEFT, RIGHT, REST = pl.ds(0, 16), pl.ds(144, 16), pl.ds(160, 16)
N_COPIES = 42
QUERY, KEY, VALUE, OUT, CQUERY, CKEY, CVALUE, COUT = range(8)


def layer(
    tok_ref, mask_ref, emb_ref, wq_ref, wk_ref, wv_ref, wo_ref, cwq_ref, cwk_ref, cwv_ref, cwo_ref,
    w1_ref, w2_ref, ones_ref, qt_ref, kt_ref, scale_ref, cscale_ref, out_ref,
    tok_s, mask_s, w_s, w1_s, w2_s, out_s, fine_s,
    buf, ls_s, rs_s, lr_s, rr_s, corner_s, up_buf, dn_buf, q_s, k_s, v_s, ku_s, vu_s, kd_s, vd_s, o_s, l_s, m_s,
    psum, cin_s, cq_s, x_s, ck_s, cv_s, qz_s, po_s, ps_s, rz_s, rst_s, fb_s, c_ref, cc_ref,
    send_sem, recv_sem, load_sem, store_sem,
):
    t, r = lax.axis_index("tile"), lax.axis_index("region")
    prev, following = (t + 31) % 32, (t + 1) % 32
    left, right = (r + 3) % 4, (r + 1) % 4
    g, z_lo = t // 2, t % 2
    z_hi, core = r // 2, r % 2
    z = 2 * z_hi + z_lo

    def plane(step):
        return {"tile": 2 * ((g + step) % 16) + z_lo, "region": r}

    def column(step):
        other = (z + step) % 4
        return {"tile": 2 * g + other % 2, "region": 2 * (other // 2) + core}

    def copy(src, dst, index, where):
        return pltpu.make_async_remote_copy(
            src_ref=src, dst_ref=dst, send_sem=send_sem.at[index], recv_sem=recv_sem.at[index],
            device_id=where, device_id_type=MESH,
        )

    load_tok = pltpu.make_async_copy(tok_ref, tok_s, load_sem.at[0])
    load_tok.start()
    names = (wq_ref, wk_ref, wv_ref, wo_ref, cwq_ref, cwk_ref, cwv_ref, cwo_ref)
    loads = [pltpu.make_async_copy(ref, w_s.at[i], load_sem.at[1 + i]) for i, ref in enumerate(names)]
    load_1 = pltpu.make_async_copy(w1_ref, w1_s, load_sem.at[9])
    load_2 = pltpu.make_async_copy(w2_ref, w2_s, load_sem.at[10])
    for i in (CQUERY, QUERY, KEY, VALUE, CKEY, CVALUE, OUT, COUT):
        loads[i].start()
    load_1.start()
    load_2.start()

    barrier = pltpu.get_barrier_semaphore()
    to_left, to_right = {"tile": t, "region": left}, {"tile": t, "region": right}
    for where in [to_left, to_right] + [{"tile": a, "region": b} for a in (prev, following) for b in (left, r, right)]:
        pl.semaphore_signal(barrier, inc=1, device_id=where, device_id_type=MESH)

    @pl.loop(1, 16)
    def _(step):
        pl.semaphore_signal(barrier, inc=1, device_id=plane(step), device_id_type=MESH)

    for step in (1, 2, 3):
        pl.semaphore_signal(barrier, inc=1, device_id=column(step), device_id_type=MESH)

    ones = ones_ref[...]
    for h in range(HEADS):
        c_ref[h] = scale_ref[h] * FACTOR
        cc_ref[h] = cscale_ref[h] * FACTOR
    psum[...] = jnp.zeros_like(psum)
    up_buf[0] = jnp.zeros((176, 512), BF16)
    dn_buf[7] = jnp.zeros((176, 512), BF16)
    up_buf[:, REST, :] = jnp.zeros((8, 16, 512), BF16)
    dn_buf[:, REST, :] = jnp.zeros((8, 16, 512), BF16)
    load_tok.wait()

    @pl.loop(0, 8)
    def _(i):
        pair = []
        for s in range(2):
            row = 2 * i + s
            m = jnp.broadcast_to(mask_ref[pl.ds(row, 1), :].astype(F32), (128, 128)).T.astype(BF16)
            mask_s[row] = m
            n = normalize(stream_of(tok_s[row], m, emb_ref[...]))
            nb = n.astype(BF16)
            buf[row] = nb
            psum[i // 4] += nb.astype(F32)
            pair.append(n)
        at = pl.ds(pl.multiple_of(16 * i, 16), 16)
        ls_s[at, :] = jnp.concatenate([n[:8] for n in pair], axis=0).astype(BF16)
        rs_s[at, :] = jnp.concatenate([n[120:] for n in pair], axis=0).astype(BF16)

    cin = normalize(jnp.sum(psum[...].reshape(32, 8, 512), axis=1) * (1.0 / 64.0)).astype(BF16)
    cin_s[...] = cin
    x_s[core, g] = cin

    pl.semaphore_wait(barrier, 26)

    sides = [copy(ls_s, rr_s, 0, to_left), copy(rs_s, lr_s, 1, to_right)]
    first, last = pl.ds(0, 64), pl.ds(64, 64)
    corners = [
        copy(rs_s.at[first, :], corner_s.at[0], 2, {"tile": prev, "region": right}),
        copy(rs_s.at[last, :], corner_s.at[1], 3, {"tile": following, "region": right}),
        copy(ls_s.at[first, :], corner_s.at[2], 4, {"tile": prev, "region": left}),
        copy(ls_s.at[last, :], corner_s.at[3], 5, {"tile": following, "region": left}),
    ]

    def row_piece(k):
        src = pl.ds(pl.multiple_of(32 * k, 16), 32)
        dst = pl.ds(pl.multiple_of(16 + 32 * k, 16), 32)
        return (
            copy(buf.at[pl.ds(0, 7), src, :], dn_buf.at[pl.ds(0, 7), dst, :], 6 + k, {"tile": prev, "region": r}),
            copy(buf.at[pl.ds(9, 7), src, :], up_buf.at[pl.ds(1, 7), dst, :], 10 + k, {"tile": following, "region": r}),
        )

    def gather(step):
        return copy(cin_s, x_s.at[core, g], 13 + step, plane(step))

    for c in sides:
        c.start()

    @pl.loop(1, 16)
    def _(step):
        gather(step).start()

    for c in corners[:2]:
        c.start()

    @pl.loop(0, 4)
    def _(k):
        for c in row_piece(k):
            c.start()

    for c in corners[2:]:
        c.start()

    loads[CQUERY].wait()
    cq = head_norm(mm(cin, w_s[CQUERY]), ones)
    cq_s[...] = cq
    qz_s[z] = cq
    asks = [copy(cq_s, qz_s.at[z], 28 + step, column(step)) for step in (1, 2, 3)]
    for c in asks:
        c.start()

    loads[QUERY].wait()

    @pl.loop(0, 4)
    def _(i):
        rows = pl.ds(4 * i, 4)
        q_s[rows] = head_norm(mm(buf[rows].reshape(512, 512), w_s[QUERY]), ones).reshape(4, 128, 512)

    loads[KEY].wait()
    loads[VALUE].wait()
    for c in sides:
        c.wait_recv()

    @pl.loop(0, 4)
    def _(i):
        rows = pl.ds(4 * i, 4)
        at = pl.ds(pl.multiple_of(32 * i, 32), 32)
        near = [ref[at, :].astype(F32).reshape(4, 8, 512) for ref in (lr_s, rr_s)]
        n = jnp.concatenate([near[0], buf[rows].astype(F32), near[1]], axis=1).astype(BF16)
        keys, vals = project(n.reshape(576, 512), w_s[KEY], w_s[VALUE], ones)
        k_s[rows] = keys.reshape(4, 144, 512)
        v_s[rows] = vals.reshape(4, 144, 512)

    @pl.loop(1, 16)
    def _(step):
        gather(step).wait_recv()

    sibling = copy(x_s.at[core], x_s.at[core], 32, {"tile": t, "region": 2 * z_hi + 1 - core})
    sibling.start()
    replies = []
    for step in (1, 2, 3):
        rows = pl.ds(pl.multiple_of(32 * ((z + step) % 4), 32), 32)
        replies.append(copy(po_s.at[rows, :], rz_s.at[z], 32 + step, column(step)))
        replies.append(copy(ps_s.at[:, rows, :], rst_s.at[z], 35 + step, column(step)))

    @pl.loop(0, 8)
    def _(j):
        @pl.when(j == 3)
        def _():
            sibling.wait_recv()
            for c in asks:
                c.wait_recv()
            loads[CKEY].wait()
            loads[CVALUE].wait()
            coarse_part(x_s, qz_s, w_s, cc_ref, ones, ck_s, cv_s, po_s, ps_s)
            for c in replies:
                c.start()
            mine = pl.ds(pl.multiple_of(32 * z, 32), 32)
            rz_s[z] = po_s[mine, :]
            rst_s[z] = ps_s[:, mine, :]

        for p in range(4):
            attend_own(j, p, q_s, k_s, v_s, qt_ref, kt_ref, c_ref, o_s, l_s, m_s)

    for c in replies:
        c.wait_recv()
    loads[COUT].wait()
    feedback = mm(coarse_join(rz_s, rst_s), w_s[COUT])
    fb_s[...] = jnp.broadcast_to(feedback.reshape(32, 1, 512), (32, 8, 512)).reshape(2, 16, 8, 512)
    loads[OUT].wait()
    load_1.wait()
    load_2.wait()

    def place(source, dst, where):
        x = source.astype(F32).reshape(8, 8, 512)
        zero = jnp.zeros_like(x)
        both = [zero, x] if where is LEFT else [x, zero]
        dst[:, where, :] = jnp.concatenate(both, axis=1).astype(BF16)

    def attend(j):
        fine = [
            attend_all(j, p, q_s, ku_s, kd_s, vu_s, vd_s, qt_ref, kt_ref, c_ref, o_s, l_s, m_s)
            for p in range(4)
        ]
        at = pl.ds(pl.multiple_of(16 * j, 16), 16)
        fine_s[:, at, :] = jnp.concatenate(fine, axis=1).reshape(16, 16, 512)

    def store(start, cols, index):
        at = pl.ds(pl.multiple_of(start, 16), cols)
        return pltpu.make_async_copy(out_s.at[:, at, :], out_ref.at[:, at, :], store_sem.at[index])

    def close(start, cols, index):
        finish(start, cols, fine_s, tok_s, mask_s, emb_ref, fb_s, w_s[OUT], w1_s, w2_s, out_s)
        store(start, cols, index).start()

    @pl.loop(0, 5)
    def _(i):
        @pl.when(i < 4)
        def _():
            for c in row_piece(i):
                c.wait_recv()

        @pl.when(i == 0)
        def _():
            for c in corners[:2]:
                c.wait_recv()
            place(corner_s[0], dn_buf, LEFT)
            place(corner_s[1], up_buf, LEFT)

        @pl.when(i == 4)
        def _():
            for c in corners[2:]:
                c.wait_recv()
            place(corner_s[2], dn_buf, RIGHT)
            place(corner_s[3], up_buf, RIGHT)

        src = pl.ds(pl.multiple_of(32 * i, 32), 48)
        cols = pl.ds(pl.multiple_of(32 * i, 32), 32)
        n = jnp.concatenate([b[:, src, :].astype(F32)[:, 8:40].astype(BF16) for b in (up_buf, dn_buf)], axis=0)
        keys, vals = project(n.reshape(512, 512), w_s[KEY], w_s[VALUE], ones)
        keys, vals = keys.reshape(16, 32, 512), vals.reshape(16, 32, 512)
        ku_s[:, cols, :], kd_s[:, cols, :] = keys[:8], keys[8:]
        vu_s[:, cols, :], vd_s[:, cols, :] = vals[:8], vals[8:]

        @pl.when(i > 0)
        def _():
            attend(2 * i - 1)

        @pl.when(i < 4)
        def _():
            attend(2 * i)

        @pl.when(i == 0)
        def _():
            close(0, 16, 0)

        @pl.when((i > 0) & (i < 4))
        def _():
            close(32 * i - 16, 32, i)

        @pl.when(i == 4)
        def _():
            close(112, 16, 4)

    store(0, 16, 0).wait()

    @pl.loop(1, 4)
    def _(i):
        store(32 * i - 16, 32, i).wait()

    store(112, 16, 4).wait()
    for c in sides + corners + asks + [sibling] + replies:
        c.wait_send()

    @pl.loop(0, 4)
    def _(k):
        for c in row_piece(k):
            c.wait_send()

    @pl.loop(1, 16)
    def _(step):
        gather(step).wait_send()


def coarse_part(x_s, qz_s, w_s, cc_ref, ones, ck_s, cv_s, po_s, ps_s):
    @pl.loop(0, 2)
    def _(i):
        x = x_s[i].reshape(512, 512)
        rows = pl.ds(pl.multiple_of(512 * i, 512), 512)
        k, v = project(x, w_s[CKEY], w_s[CVALUE], ones)
        ck_s[rows, :] = k
        cv_s[rows, :] = v

    q = qz_s[...].reshape(128, 512)
    lane = lax.broadcasted_iota(jnp.int32, (128, 128), 1)
    head = lax.broadcasted_iota(jnp.int32, (128, 256), 1) // 64
    tops = jnp.zeros((128, 128), F32)
    sums = jnp.zeros((128, 128), F32)
    for half in range(2):
        lanes = slice(256 * half, 256 * half + 256)
        qh = q[:, lanes]
        rows = jnp.concatenate([jnp.where(head == h, qh, jnp.zeros_like(qh)) for h in range(4)], axis=0)
        s = lax.dot_general(rows, ck_s[:, lanes], NT, preferred_element_type=F32)
        weights = []
        for h in range(4):
            c = cc_ref[4 * half + h]
            part = s[128 * h : 128 * h + 128]
            top = jnp.max(part, axis=-1, keepdims=True)
            w = jnp.exp2((part - top) * c)
            tops = jnp.where(lane == 4 * half + h, top * c, tops)
            sums = jnp.where(lane == 4 * half + h, jnp.sum(w, axis=-1, keepdims=True), sums)
            weights.append(w.astype(BF16))
        o = mm(jnp.concatenate(weights, axis=0), cv_s[:, lanes])
        picked = o[:128]
        for h in range(1, 4):
            picked = jnp.where(head == h, o[128 * h : 128 * h + 128], picked)
        po_s[:, lanes] = picked
    ps_s[0] = tops
    ps_s[1] = sums


def coarse_join(rz_s, rs_s):
    top = jnp.maximum(jnp.maximum(rs_s[0, 0], rs_s[1, 0]), jnp.maximum(rs_s[2, 0], rs_s[3, 0]))
    scale = [jnp.exp2(rs_s[i, 0] - top) for i in range(4)]
    total = sum(scale[i] * rs_s[i, 1] for i in range(4))
    low = lax.broadcasted_iota(jnp.int32, (32, 128), 1) < 64
    joined = jnp.zeros((32, 512), F32)
    for i in range(4):
        a = scale[i] / total
        wide = [
            jnp.where(low, jnp.broadcast_to(a[:, 2 * p : 2 * p + 1], (32, 128)), jnp.broadcast_to(a[:, 2 * p + 1 : 2 * p + 2], (32, 128)))
            for p in range(4)
        ]
        joined = joined + jnp.concatenate(wide, axis=1) * rz_s[i]
    return joined.astype(BF16)


def body(
    tokens, pore_mask, solid_embed, fine_query, fine_key, fine_value, fine_out, fine_scale,
    coarse_query, coarse_key, coarse_value, coarse_out, coarse_scale, mlp_in, mlp_out,
):
    vm = pl.BlockSpec(memory_space=pltpu.VMEM)
    sm = pl.BlockSpec(memory_space=pltpu.SMEM)
    hbm = pl.BlockSpec(memory_space=pl.ANY)

    def half(*shape):
        return pltpu.VMEM(shape, BF16)

    def full(*shape):
        return pltpu.VMEM(shape, F32)

    dma = pltpu.SemaphoreType.DMA
    return pl.pallas_call(
        layer,
        out_shape=jax.ShapeDtypeStruct((16, 128, 512), BF16),
        in_specs=[hbm, vm, vm] + [hbm] * 10 + [vm] * 3 + [sm] * 2,
        out_specs=hbm,
        scratch_shapes=[
            half(16, 128, 512),
            half(16, 128, 128),
            half(8, 512, 512),
            half(512, 2048),
            half(2048, 512),
            half(16, 128, 512),
            half(16, 128, 512),
            half(16, 128, 512),
            half(128, 512),
            half(128, 512),
            half(128, 512),
            half(128, 512),
            half(4, 64, 512),
            half(8, 176, 512),
            half(8, 176, 512),
            half(16, 128, 512),
            half(16, 144, 512),
            half(16, 144, 512),
            half(8, 160, 512),
            half(8, 160, 512),
            half(8, 160, 512),
            half(8, 160, 512),
            full(8, 4, 256, 128),
            full(8, 4, 256, 128),
            full(8, 4, 256, 128),
            full(2, 128, 512),
            half(32, 512),
            half(32, 512),
            half(2, 16, 32, 512),
            half(1024, 512),
            half(1024, 512),
            half(4, 32, 512),
            full(128, 512),
            full(2, 128, 128),
            full(4, 32, 512),
            full(4, 2, 32, 128),
            full(2, 16, 8, 512),
            pltpu.SMEM((8,), F32),
            pltpu.SMEM((8,), F32),
            dma((N_COPIES,)),
            dma((N_COPIES,)),
            dma((11,)),
            dma((5,)),
        ],
        compiler_params=pltpu.CompilerParams(
            collective_id=0, has_side_effects=True, vmem_limit_bytes=62 * 2**20
        ),
    )(
        tokens, pore_mask, solid_embed.reshape(1, 512), fine_query, fine_key, fine_value, fine_out,
        coarse_query, coarse_key, coarse_value, coarse_out, mlp_in, mlp_out,
        block_ones(), query_table(), key_tables(), fine_scale, coarse_scale,
    )


def solution(mesh):
    placed = (P("tile", "region", None), P("tile", "region")) + (P(),) * 13
    return jax.shard_map(
        body, mesh=mesh, in_specs=placed, out_specs=P("tile", "region", None), check_vma=False
    )
```

```python
import functools
import math

import jax
import jax.numpy as jnp
import numpy as np
from jax import lax
from jax.experimental import pallas as pl
from jax.experimental.pallas import tpu as pltpu
from jax.sharding import PartitionSpec as P

F32, BF16 = jnp.float32, jnp.bfloat16
MESH = pl.DeviceIdType.MESH
HEADS = 8
EPS = 1e-6
BIG = 131072.0
FACTOR = math.log2(math.e) / 8.0
TAIL = (
    -1.0002404059668364,
    -1.1475987944049173,
    -0.46737700467532134,
    -0.04592394901048988,
    0.005166375711832039,
    -0.00025544077122896525,
)
NT = (((1,), (1,)), ((), ()))


def mm(a, b):
    return jnp.dot(a, b, preferred_element_type=F32)


def gelu(x):
    x = x.astype(BF16)
    z = jnp.abs(x)
    p = z * BF16(TAIL[5]) + BF16(TAIL[4])
    for c in TAIL[3::-1]:
        p = p * z + BF16(c)
    return jnp.maximum(x, BF16(0)) - z * jnp.exp2(p)


def block_ones():
    i = np.arange(256) // 64
    return jnp.asarray((i[:, None] == i[None, :]).astype(np.float32) / 64.0, BF16)


def key_tables():
    t = np.zeros((4, 8, 32, 128), np.float32)
    q = np.arange(16)
    for chunk in range(4):
        for row in range(8):
            away = np.abs(q - (8 * (chunk - 1) + row))
            t[chunk, row, :, 0:16] = np.where(away <= 7, 0.0, -BIG)[None, :]
        for col in range(32):
            t[chunk, :, col, 16:32] = np.where(np.abs(q - (col - 8)) <= 7, 0.0, -BIG)[None, :]
    return jnp.asarray(t.reshape(4, 256, 128), BF16)


def query_table():
    t = np.zeros((16, 16, 128), np.float32)
    for i in range(16):
        t[i, :, i] = 1.0
        t[:, i, 16 + i] = 1.0
    return jnp.asarray(t.reshape(256, 128), BF16)


def head_norm(p, ones):
    sq = (p * p).astype(BF16)
    ms = jnp.concatenate([mm(sq[:, :256], ones), mm(sq[:, 256:], ones)], axis=1)
    return (p * lax.rsqrt(ms + EPS)).astype(BF16)


def normalize(x):
    return x * lax.rsqrt(jnp.mean(x * x, axis=-1, keepdims=True) + EPS)


def queries_of(q_s, qt_ref, j, p):
    q = q_s[:, pl.ds(pl.multiple_of(16 * j, 16), 16), 128 * p : 128 * p + 128].reshape(256, 128)
    low = lax.broadcasted_iota(jnp.int32, (256, 128), 1) < 64
    zero = jnp.zeros_like(q)
    qt = qt_ref[...]
    return [
        jnp.concatenate([jnp.where(low, q, zero), qt], axis=1),
        jnp.concatenate([jnp.where(low, zero, q), qt], axis=1),
    ]


def chunk_of(ref, row, j, p, extra):
    cols = pl.ds(pl.multiple_of(16 * j, 16), 32)
    x = ref[row : row + 8, cols, 128 * p : 128 * p + 128].reshape(256, 128)
    return jnp.concatenate([x, extra], axis=1)


def soft(s, c):
    top = jnp.max(s, axis=-1, keepdims=True)
    return jnp.exp2((s - top) * c).astype(BF16), top * c


def merge(first, second):
    low = lax.broadcasted_iota(jnp.int32, first.shape, 1) < 64
    return jnp.where(low, first, second)


def attend_own(j, p, q_s, k_s, v_s, qt_ref, kt_ref, c_ref, o_s, l_s, m_s):
    qa, qb = queries_of(q_s, qt_ref, j, p)
    ones = jnp.ones((256, 128), BF16)
    keys = jnp.concatenate([chunk_of(k_s, 8 * i, j, p, kt_ref[1 + i]) for i in range(2)], axis=0)
    vals = jnp.concatenate([chunk_of(v_s, 8 * i, j, p, ones) for i in range(2)], axis=0)
    s = lax.dot_general(jnp.concatenate([qa, qb], axis=0), keys, NT, preferred_element_type=F32)
    wa, ma = soft(s[:256], c_ref[2 * p])
    wb, mb = soft(s[256:], c_ref[2 * p + 1])
    o = mm(jnp.concatenate([wa, wb], axis=0), vals)
    o_s[j, p] = merge(o[:256, :128], o[256:, :128])
    l_s[j, p] = merge(o[:256, 128:], o[256:, 128:])
    m_s[j, p] = merge(jnp.broadcast_to(ma, (256, 128)), jnp.broadcast_to(mb, (256, 128)))


def attend_all(j, p, q_s, ku_s, kd_s, vu_s, vd_s, qt_ref, kt_ref, c_ref, o_s, l_s, m_s):
    qa, qb = queries_of(q_s, qt_ref, j, p)
    ones = jnp.ones((256, 128), BF16)
    done = []
    for k_s, v_s, table, part in ((ku_s, vu_s, 0, slice(0, 128)), (kd_s, vd_s, 3, slice(128, 256))):
        keys = chunk_of(k_s, 0, j, p, kt_ref[table])
        vals = chunk_of(v_s, 0, j, p, ones)
        q = jnp.concatenate([qa[part], qb[part]], axis=0)
        s = lax.dot_general(q, keys, NT, preferred_element_type=F32)
        wa, ma = soft(s[:128], c_ref[2 * p])
        wb, mb = soft(s[128:], c_ref[2 * p + 1])
        o = mm(jnp.concatenate([wa, wb], axis=0), vals)
        o2 = merge(o[:128, :128], o[128:, :128])
        l2 = merge(o[:128, 128:], o[128:, 128:])
        m2 = merge(jnp.broadcast_to(ma, (128, 128)), jnp.broadcast_to(mb, (128, 128)))
        o1, l1, m1 = o_s[j, p, part], l_s[j, p, part], m_s[j, p, part]
        top = jnp.maximum(m1, m2)
        a1, a2 = jnp.exp2(m1 - top), jnp.exp2(m2 - top)
        done.append(((o1 * a1 + o2 * a2) / (l1 * a1 + l2 * a2)).astype(BF16))
    return jnp.concatenate(done, axis=0)


def project(n, wk, wv, ones):
    return head_norm(mm(n, wk), ones), mm(n, wv).astype(BF16)


def stream_of(tok, mask, emb):
    m = mask.astype(F32)
    return tok.astype(F32) + jnp.concatenate([m] * 4, axis=1) * emb


def finish(start, cols, fine_s, tok_s, mask_s, emb_ref, fb_s, wo, w1_s, w2_s, out_s):
    count = 16 * cols
    at = pl.ds(pl.multiple_of(start, 16), cols)
    stream = stream_of(tok_s[:, at, :].reshape(count, 512), mask_s[:, at, :].reshape(count, 128), emb_ref[...])
    fb = fb_s[:, pl.ds(start // 8, cols // 8)].reshape(2, 1, cols, 512)
    fb = jnp.broadcast_to(fb, (2, 8, cols, 512)).reshape(count, 512)
    mixed = stream + mm(fine_s[:, at, :].reshape(count, 512), wo) + fb
    nm = normalize(mixed).astype(BF16)
    acc = mixed
    ahead = mm(nm, w1_s[:, :512])
    for f in range(4):
        now = ahead
        if f < 3:
            ahead = mm(nm, w1_s[:, 512 * f + 512 : 512 * f + 1024])
        acc = acc + mm(gelu(now), w2_s[512 * f : 512 * f + 512, :])
    out_s[:, at, :] = acc.astype(BF16).reshape(16, cols, 512)


LEFT, RIGHT, REST = pl.ds(0, 16), pl.ds(144, 16), pl.ds(160, 16)
N_COPIES = 42
QUERY, KEY, VALUE, OUT, CQUERY, CKEY, CVALUE, COUT = range(8)


def layer(
    tok_ref, mask_ref, emb_ref, wq_ref, wk_ref, wv_ref, wo_ref, cwq_ref, cwk_ref, cwv_ref, cwo_ref,
    w1_ref, w2_ref, ones_ref, qt_ref, kt_ref, scale_ref, cscale_ref, out_ref,
    tok_s, mask_s, w_s, w1_s, w2_s, out_s, fine_s,
    buf, ls_s, rs_s, lr_s, rr_s, corner_s, up_buf, dn_buf, q_s, k_s, v_s, ku_s, vu_s, kd_s, vd_s, o_s, l_s, m_s,
    psum, cin_s, cq_s, x_s, ck_s, cv_s, qz_s, po_s, ps_s, rz_s, rst_s, fb_s, c_ref, cc_ref,
    send_sem, recv_sem, load_sem, store_sem,
):
    t, r = lax.axis_index("tile"), lax.axis_index("region")
    prev, following = (t + 31) % 32, (t + 1) % 32
    left, right = (r + 3) % 4, (r + 1) % 4
    g, z_lo = t // 2, t % 2
    z_hi, core = r // 2, r % 2
    z = 2 * z_hi + z_lo

    def plane(step):
        return {"tile": 2 * ((g + step) % 16) + z_lo, "region": r}

    def column(step):
        other = (z + step) % 4
        return {"tile": 2 * g + other % 2, "region": 2 * (other // 2) + core}

    def copy(src, dst, index, where):
        return pltpu.make_async_remote_copy(
            src_ref=src, dst_ref=dst, send_sem=send_sem.at[index], recv_sem=recv_sem.at[index],
            device_id=where, device_id_type=MESH,
        )

    load_tok = pltpu.make_async_copy(tok_ref, tok_s, load_sem.at[0])
    load_tok.start()
    names = (wq_ref, wk_ref, wv_ref, wo_ref, cwq_ref, cwk_ref, cwv_ref, cwo_ref)
    loads = [pltpu.make_async_copy(ref, w_s.at[i], load_sem.at[1 + i]) for i, ref in enumerate(names)]
    load_1 = pltpu.make_async_copy(w1_ref, w1_s, load_sem.at[9])
    load_2 = pltpu.make_async_copy(w2_ref, w2_s, load_sem.at[10])
    for i in (CQUERY, QUERY, KEY, VALUE, CKEY, CVALUE, OUT, COUT):
        loads[i].start()
    load_1.start()
    load_2.start()

    barrier = pltpu.get_barrier_semaphore()
    to_left, to_right = {"tile": t, "region": left}, {"tile": t, "region": right}
    for where in [to_left, to_right] + [{"tile": a, "region": b} for a in (prev, following) for b in (left, r, right)]:
        pl.semaphore_signal(barrier, inc=1, device_id=where, device_id_type=MESH)

    @pl.loop(1, 16)
    def _(step):
        pl.semaphore_signal(barrier, inc=1, device_id=plane(step), device_id_type=MESH)

    for step in (1, 2, 3):
        pl.semaphore_signal(barrier, inc=1, device_id=column(step), device_id_type=MESH)

    ones = ones_ref[...]
    for h in range(HEADS):
        c_ref[h] = scale_ref[h] * FACTOR
        cc_ref[h] = cscale_ref[h] * FACTOR
    psum[...] = jnp.zeros_like(psum)
    up_buf[0] = jnp.zeros((176, 512), BF16)
    dn_buf[7] = jnp.zeros((176, 512), BF16)
    up_buf[:, REST, :] = jnp.zeros((8, 16, 512), BF16)
    dn_buf[:, REST, :] = jnp.zeros((8, 16, 512), BF16)
    load_tok.wait()

    def norm_rows(i):
        lo, hi = [], []
        total = jnp.zeros((128, 512), F32)
        for k in range(4):
            row = 4 * i + k
            m = jnp.broadcast_to(mask_ref[pl.ds(row, 1), :].astype(F32), (128, 128)).T.astype(BF16)
            mask_s[row] = m
            n = normalize(stream_of(tok_s[row], m, emb_ref[...]))
            nb = n.astype(BF16)
            buf[row] = nb
            total = total + nb.astype(F32)
            lo.append(n[:8])
            hi.append(n[120:])
        psum[i // 2] += total
        at = pl.ds(pl.multiple_of(32 * i, 32), 32)
        ls_s[at, :] = jnp.concatenate(lo, axis=0).astype(BF16)
        rs_s[at, :] = jnp.concatenate(hi, axis=0).astype(BF16)

    sides = [copy(ls_s, rr_s, 0, to_left), copy(rs_s, lr_s, 1, to_right)]
    first, last = pl.ds(0, 64), pl.ds(64, 64)
    corners = [
        copy(rs_s.at[first, :], corner_s.at[0], 2, {"tile": prev, "region": right}),
        copy(rs_s.at[last, :], corner_s.at[1], 3, {"tile": following, "region": right}),
        copy(ls_s.at[first, :], corner_s.at[2], 4, {"tile": prev, "region": left}),
        copy(ls_s.at[last, :], corner_s.at[3], 5, {"tile": following, "region": left}),
    ]

    def row_piece(k):
        src = pl.ds(pl.multiple_of(32 * k, 16), 32)
        dst = pl.ds(pl.multiple_of(16 + 32 * k, 16), 32)
        return (
            copy(buf.at[pl.ds(0, 7), src, :], dn_buf.at[pl.ds(0, 7), dst, :], 6 + k, {"tile": prev, "region": r}),
            copy(buf.at[pl.ds(9, 7), src, :], up_buf.at[pl.ds(1, 7), dst, :], 10 + k, {"tile": following, "region": r}),
        )

    @pl.loop(0, 2)
    def _(i):
        norm_rows(i)

    pl.semaphore_wait(barrier, 26)
    row_piece(0)[0].start()

    @pl.loop(2, 4)
    def _(i):
        norm_rows(i)

    row_piece(0)[1].start()
    for c in sides:
        c.start()
    cin = normalize(jnp.sum(psum[...].reshape(32, 8, 512), axis=1) * (1.0 / 64.0)).astype(BF16)
    cin_s[...] = cin
    x_s[core, g] = cin

    def gather(step):
        return copy(cin_s, x_s.at[core, g], 13 + step, plane(step))

    @pl.loop(1, 16)
    def _(step):
        gather(step).start()

    for c in row_piece(1):
        c.start()
    for c in corners[:2]:
        c.start()

    loads[CQUERY].wait()
    cq = head_norm(mm(cin, w_s[CQUERY]), ones)
    cq_s[...] = cq
    qz_s[z] = cq
    asks = [copy(cq_s, qz_s.at[z], 28 + step, column(step)) for step in (1, 2, 3)]
    for c in asks:
        c.start()

    loads[QUERY].wait()

    @pl.loop(0, 4)
    def _(i):
        rows = pl.ds(4 * i, 4)
        q_s[rows] = head_norm(mm(buf[rows].reshape(512, 512), w_s[QUERY]), ones).reshape(4, 128, 512)

    loads[KEY].wait()
    loads[VALUE].wait()
    for c in sides:
        c.wait_recv()

    @pl.loop(0, 4)
    def _(i):
        rows = pl.ds(4 * i, 4)
        at = pl.ds(pl.multiple_of(32 * i, 32), 32)
        near = [ref[at, :].astype(F32).reshape(4, 8, 512) for ref in (lr_s, rr_s)]
        n = jnp.concatenate([near[0], buf[rows].astype(F32), near[1]], axis=1).astype(BF16)
        keys, vals = project(n.reshape(576, 512), w_s[KEY], w_s[VALUE], ones)
        k_s[rows] = keys.reshape(4, 144, 512)
        v_s[rows] = vals.reshape(4, 144, 512)

    @pl.loop(1, 16)
    def _(step):
        gather(step).wait_recv()

    sibling = copy(x_s.at[core], x_s.at[core], 32, {"tile": t, "region": 2 * z_hi + 1 - core})
    sibling.start()
    replies = []
    for step in (1, 2, 3):
        rows = pl.ds(pl.multiple_of(32 * ((z + step) % 4), 32), 32)
        replies.append(copy(po_s.at[rows, :], rz_s.at[z], 32 + step, column(step)))
        replies.append(copy(ps_s.at[:, rows, :], rst_s.at[z], 35 + step, column(step)))

    @pl.loop(0, 4)
    def _(j):
        @pl.when(j == 2)
        def _():
            sibling.wait_recv()
            for c in asks:
                c.wait_recv()
            loads[CKEY].wait()
            loads[CVALUE].wait()
            coarse_part(x_s, qz_s, w_s, cc_ref, ones, ck_s, cv_s, po_s, ps_s)
            for c in replies:
                c.start()
            mine = pl.ds(pl.multiple_of(32 * z, 32), 32)
            rz_s[z] = po_s[mine, :]
            rst_s[z] = ps_s[:, mine, :]

        for p in range(8):
            attend_own(2 * j + p // 4, p % 4, q_s, k_s, v_s, qt_ref, kt_ref, c_ref, o_s, l_s, m_s)

    for c in row_piece(0):
        c.wait_send()
    for c in row_piece(2):
        c.start()
    for c in replies:
        c.wait_recv()
    loads[COUT].wait()
    feedback = mm(coarse_join(rz_s, rst_s), w_s[COUT])
    fb_s[...] = jnp.broadcast_to(feedback.reshape(32, 1, 512), (32, 8, 512)).reshape(2, 16, 8, 512)
    loads[OUT].wait()
    load_1.wait()
    load_2.wait()

    def place(source, dst, where):
        x = source.astype(F32).reshape(8, 8, 512)
        zero = jnp.zeros_like(x)
        both = [zero, x] if where is LEFT else [x, zero]
        dst[:, where, :] = jnp.concatenate(both, axis=1).astype(BF16)

    def attend(j):
        fine = [
            attend_all(j, p, q_s, ku_s, kd_s, vu_s, vd_s, qt_ref, kt_ref, c_ref, o_s, l_s, m_s)
            for p in range(4)
        ]
        at = pl.ds(pl.multiple_of(16 * j, 16), 16)
        fine_s[:, at, :] = jnp.concatenate(fine, axis=1).reshape(16, 16, 512)

    def store(start, cols, index):
        at = pl.ds(pl.multiple_of(start, 16), cols)
        return pltpu.make_async_copy(out_s.at[:, at, :], out_ref.at[:, at, :], store_sem.at[index])

    def close(start, cols, index):
        finish(start, cols, fine_s, tok_s, mask_s, emb_ref, fb_s, w_s[OUT], w1_s, w2_s, out_s)
        store(start, cols, index).start()

    @pl.loop(0, 5)
    def _(i):
        @pl.when(i < 4)
        def _():
            for c in row_piece(i):
                c.wait_recv()

        @pl.when(i == 0)
        def _():
            for c in corners[:2]:
                c.wait_recv()
            place(corner_s[0], dn_buf, LEFT)
            place(corner_s[1], up_buf, LEFT)

        @pl.when(i == 4)
        def _():
            for c in corners[2:]:
                c.wait_recv()
            place(corner_s[2], dn_buf, RIGHT)
            place(corner_s[3], up_buf, RIGHT)

        src = pl.ds(pl.multiple_of(32 * i, 32), 48)
        cols = pl.ds(pl.multiple_of(32 * i, 32), 32)
        n = jnp.concatenate([b[:, src, :].astype(F32)[:, 8:40].astype(BF16) for b in (up_buf, dn_buf)], axis=0)
        keys, vals = project(n.reshape(512, 512), w_s[KEY], w_s[VALUE], ones)
        keys, vals = keys.reshape(16, 32, 512), vals.reshape(16, 32, 512)
        ku_s[:, cols, :], kd_s[:, cols, :] = keys[:8], keys[8:]
        vu_s[:, cols, :], vd_s[:, cols, :] = vals[:8], vals[8:]

        @pl.when(i == 0)
        def _():
            attend(0)
            close(0, 16, 0)

        @pl.when(i == 1)
        def _():
            for c in row_piece(1):
                c.wait_send()
            for c in row_piece(3) + tuple(corners[2:]):
                c.start()

        @pl.when((i > 0) & (i < 4))
        def _():
            attend(2 * i - 1)
            attend(2 * i)
            close(32 * i - 16, 32, i)

        @pl.when(i == 4)
        def _():
            attend(7)
            close(112, 16, 4)

    store(0, 16, 0).wait()

    @pl.loop(1, 4)
    def _(i):
        store(32 * i - 16, 32, i).wait()

    store(112, 16, 4).wait()
    for c in sides + corners + asks + [sibling] + replies:
        c.wait_send()

    for k in (2, 3):
        for c in row_piece(k):
            c.wait_send()

    @pl.loop(1, 16)
    def _(step):
        gather(step).wait_send()


def coarse_part(x_s, qz_s, w_s, cc_ref, ones, ck_s, cv_s, po_s, ps_s):
    @pl.loop(0, 2)
    def _(i):
        x = x_s[i].reshape(512, 512)
        rows = pl.ds(pl.multiple_of(512 * i, 512), 512)
        k, v = project(x, w_s[CKEY], w_s[CVALUE], ones)
        ck_s[rows, :] = k
        cv_s[rows, :] = v

    q = qz_s[...].reshape(128, 512)
    lane = lax.broadcasted_iota(jnp.int32, (128, 128), 1)
    head = lax.broadcasted_iota(jnp.int32, (128, 256), 1) // 64
    tops = jnp.zeros((128, 128), F32)
    sums = jnp.zeros((128, 128), F32)
    for half in range(2):
        lanes = slice(256 * half, 256 * half + 256)
        qh = q[:, lanes]
        rows = jnp.concatenate([jnp.where(head == h, qh, jnp.zeros_like(qh)) for h in range(4)], axis=0)
        s = lax.dot_general(rows, ck_s[:, lanes], NT, preferred_element_type=F32)
        weights = []
        for h in range(4):
            c = cc_ref[4 * half + h]
            part = s[128 * h : 128 * h + 128]
            top = jnp.max(part, axis=-1, keepdims=True)
            w = jnp.exp2((part - top) * c)
            tops = jnp.where(lane == 4 * half + h, top * c, tops)
            sums = jnp.where(lane == 4 * half + h, jnp.sum(w, axis=-1, keepdims=True), sums)
            weights.append(w.astype(BF16))
        o = mm(jnp.concatenate(weights, axis=0), cv_s[:, lanes])
        picked = o[:128]
        for h in range(1, 4):
            picked = jnp.where(head == h, o[128 * h : 128 * h + 128], picked)
        po_s[:, lanes] = picked
    ps_s[0] = tops
    ps_s[1] = sums


def coarse_join(rz_s, rs_s):
    top = jnp.maximum(jnp.maximum(rs_s[0, 0], rs_s[1, 0]), jnp.maximum(rs_s[2, 0], rs_s[3, 0]))
    scale = [jnp.exp2(rs_s[i, 0] - top) for i in range(4)]
    total = sum(scale[i] * rs_s[i, 1] for i in range(4))
    low = lax.broadcasted_iota(jnp.int32, (32, 128), 1) < 64
    joined = jnp.zeros((32, 512), F32)
    for i in range(4):
        a = scale[i] / total
        wide = [
            jnp.where(low, jnp.broadcast_to(a[:, 2 * p : 2 * p + 1], (32, 128)), jnp.broadcast_to(a[:, 2 * p + 1 : 2 * p + 2], (32, 128)))
            for p in range(4)
        ]
        joined = joined + jnp.concatenate(wide, axis=1) * rz_s[i]
    return joined.astype(BF16)


def body(
    tokens, pore_mask, solid_embed, fine_query, fine_key, fine_value, fine_out, fine_scale,
    coarse_query, coarse_key, coarse_value, coarse_out, coarse_scale, mlp_in, mlp_out,
):
    vm = pl.BlockSpec(memory_space=pltpu.VMEM)
    sm = pl.BlockSpec(memory_space=pltpu.SMEM)
    hbm = pl.BlockSpec(memory_space=pl.ANY)

    def half(*shape):
        return pltpu.VMEM(shape, BF16)

    def full(*shape):
        return pltpu.VMEM(shape, F32)

    dma = pltpu.SemaphoreType.DMA
    return pl.pallas_call(
        layer,
        out_shape=jax.ShapeDtypeStruct((16, 128, 512), BF16),
        in_specs=[hbm, vm, vm] + [hbm] * 10 + [vm] * 3 + [sm] * 2,
        out_specs=hbm,
        scratch_shapes=[
            half(16, 128, 512),
            half(16, 128, 128),
            half(8, 512, 512),
            half(512, 2048),
            half(2048, 512),
            half(16, 128, 512),
            half(16, 128, 512),
            half(16, 128, 512),
            half(128, 512),
            half(128, 512),
            half(128, 512),
            half(128, 512),
            half(4, 64, 512),
            half(8, 176, 512),
            half(8, 176, 512),
            half(16, 128, 512),
            half(16, 144, 512),
            half(16, 144, 512),
            half(8, 160, 512),
            half(8, 160, 512),
            half(8, 160, 512),
            half(8, 160, 512),
            full(8, 4, 256, 128),
            full(8, 4, 256, 128),
            full(8, 4, 256, 128),
            full(2, 128, 512),
            half(32, 512),
            half(32, 512),
            half(2, 16, 32, 512),
            half(1024, 512),
            half(1024, 512),
            half(4, 32, 512),
            full(128, 512),
            full(2, 128, 128),
            full(4, 32, 512),
            full(4, 2, 32, 128),
            full(2, 16, 8, 512),
            pltpu.SMEM((8,), F32),
            pltpu.SMEM((8,), F32),
            dma((N_COPIES,)),
            dma((N_COPIES,)),
            dma((11,)),
            dma((5,)),
        ],
        compiler_params=pltpu.CompilerParams(
            collective_id=0, has_side_effects=True, vmem_limit_bytes=62 * 2**20
        ),
    )(
        tokens, pore_mask, solid_embed.reshape(1, 512), fine_query, fine_key, fine_value, fine_out,
        coarse_query, coarse_key, coarse_value, coarse_out, mlp_in, mlp_out,
        block_ones(), query_table(), key_tables(), fine_scale, coarse_scale,
    )


def solution(mesh):
    placed = (P("tile", "region", None), P("tile", "region")) + (P(),) * 13
    return jax.shard_map(
        body, mesh=mesh, in_specs=placed, out_specs=P("tile", "region", None), check_vma=False
    )
```

```python
import functools
import math

import jax
import jax.numpy as jnp
import numpy as np
from jax import lax
from jax.experimental import pallas as pl
from jax.experimental.pallas import tpu as pltpu
from jax.sharding import PartitionSpec as P

F32, BF16 = jnp.float32, jnp.bfloat16
MESH = pl.DeviceIdType.MESH
HEADS = 8
EPS = 1e-6
BIG = 131072.0
FACTOR = math.log2(math.e) / 8.0
TAIL = (
    -1.0002404059668364,
    -1.1475987944049173,
    -0.46737700467532134,
    -0.04592394901048988,
    0.005166375711832039,
    -0.00025544077122896525,
)
NT = (((1,), (1,)), ((), ()))


def mm(a, b):
    return jnp.dot(a, b, preferred_element_type=F32)


def gelu(x):
    x = x.astype(BF16)
    z = jnp.abs(x)
    p = z * BF16(TAIL[5]) + BF16(TAIL[4])
    for c in TAIL[3::-1]:
        p = p * z + BF16(c)
    return jnp.maximum(x, BF16(0)) - z * jnp.exp2(p)


def block_ones():
    i = np.arange(256) // 64
    return jnp.asarray((i[:, None] == i[None, :]).astype(np.float32) / 64.0, BF16)


def key_tables():
    t = np.zeros((4, 8, 32, 128), np.float32)
    q = np.arange(16)
    for chunk in range(4):
        for row in range(8):
            away = np.abs(q - (8 * (chunk - 1) + row))
            t[chunk, row, :, 0:16] = np.where(away <= 7, 0.0, -BIG)[None, :]
        for col in range(32):
            t[chunk, :, col, 16:32] = np.where(np.abs(q - (col - 8)) <= 7, 0.0, -BIG)[None, :]
    return jnp.asarray(t.reshape(4, 256, 128), BF16)


def query_table():
    t = np.zeros((16, 16, 128), np.float32)
    for i in range(16):
        t[i, :, i] = 1.0
        t[:, i, 16 + i] = 1.0
    return jnp.asarray(t.reshape(256, 128), BF16)


def head_norm(p, ones):
    sq = (p * p).astype(BF16)
    ms = jnp.concatenate([mm(sq[:, :256], ones), mm(sq[:, 256:], ones)], axis=1)
    return (p * lax.rsqrt(ms + EPS)).astype(BF16)


def normalize(x):
    return x * lax.rsqrt(jnp.mean(x * x, axis=-1, keepdims=True) + EPS)


def queries_of(q_s, qt_ref, j, p):
    q = q_s[:, pl.ds(pl.multiple_of(16 * j, 16), 16), 128 * p : 128 * p + 128].reshape(256, 128)
    low = lax.broadcasted_iota(jnp.int32, (256, 128), 1) < 64
    zero = jnp.zeros_like(q)
    qt = qt_ref[...]
    return [
        jnp.concatenate([jnp.where(low, q, zero), qt], axis=1),
        jnp.concatenate([jnp.where(low, zero, q), qt], axis=1),
    ]


def chunk_of(ref, row, j, p, extra):
    cols = pl.ds(pl.multiple_of(16 * j, 16), 32)
    x = ref[row : row + 8, cols, 128 * p : 128 * p + 128].reshape(256, 128)
    return jnp.concatenate([x, extra], axis=1)


def soft(s, c):
    top = jnp.max(s, axis=-1, keepdims=True)
    return jnp.exp2((s - top) * c).astype(BF16), top * c


def merge(first, second):
    low = lax.broadcasted_iota(jnp.int32, first.shape, 1) < 64
    return jnp.where(low, first, second)


def attend_own(j, p, q_s, k_s, v_s, qt_ref, kt_ref, c_ref, o_s, l_s, m_s):
    qa, qb = queries_of(q_s, qt_ref, j, p)
    ones = jnp.ones((256, 128), BF16)
    keys = jnp.concatenate([chunk_of(k_s, 8 * i, j, p, kt_ref[1 + i]) for i in range(2)], axis=0)
    vals = jnp.concatenate([chunk_of(v_s, 8 * i, j, p, ones) for i in range(2)], axis=0)
    s = lax.dot_general(jnp.concatenate([qa, qb], axis=0), keys, NT, preferred_element_type=F32)
    wa, ma = soft(s[:256], c_ref[2 * p])
    wb, mb = soft(s[256:], c_ref[2 * p + 1])
    o = mm(jnp.concatenate([wa, wb], axis=0), vals)
    o_s[j, p] = merge(o[:256, :128], o[256:, :128])
    l_s[j, p] = merge(o[:256, 128:], o[256:, 128:])
    m_s[j, p] = merge(jnp.broadcast_to(ma, (256, 128)), jnp.broadcast_to(mb, (256, 128)))


def attend_all(j, p, q_s, ku_s, kd_s, vu_s, vd_s, qt_ref, kt_ref, c_ref, o_s, l_s, m_s):
    qa, qb = queries_of(q_s, qt_ref, j, p)
    ones = jnp.ones((256, 128), BF16)
    done = []
    for k_s, v_s, table, part in ((ku_s, vu_s, 0, slice(0, 128)), (kd_s, vd_s, 3, slice(128, 256))):
        keys = chunk_of(k_s, 0, j, p, kt_ref[table])
        vals = chunk_of(v_s, 0, j, p, ones)
        q = jnp.concatenate([qa[part], qb[part]], axis=0)
        s = lax.dot_general(q, keys, NT, preferred_element_type=F32)
        wa, ma = soft(s[:128], c_ref[2 * p])
        wb, mb = soft(s[128:], c_ref[2 * p + 1])
        o = mm(jnp.concatenate([wa, wb], axis=0), vals)
        o2 = merge(o[:128, :128], o[128:, :128])
        l2 = merge(o[:128, 128:], o[128:, 128:])
        m2 = merge(jnp.broadcast_to(ma, (128, 128)), jnp.broadcast_to(mb, (128, 128)))
        o1, l1, m1 = o_s[j, p, part], l_s[j, p, part], m_s[j, p, part]
        top = jnp.maximum(m1, m2)
        a1, a2 = jnp.exp2(m1 - top), jnp.exp2(m2 - top)
        done.append(((o1 * a1 + o2 * a2) / (l1 * a1 + l2 * a2)).astype(BF16))
    return jnp.concatenate(done, axis=0)


def project(n, wk, wv, ones):
    return head_norm(mm(n, wk), ones), mm(n, wv).astype(BF16)


def stream_of(tok, mask, emb):
    m = mask.astype(F32)
    return tok.astype(F32) + jnp.concatenate([m] * 4, axis=1) * emb


def finish(start, cols, fine_s, tok_s, mask_s, emb_ref, fb_s, wo, w1_s, w2_s, out_s):
    count = 16 * cols
    at = pl.ds(pl.multiple_of(start, 16), cols)
    stream = stream_of(tok_s[:, at, :].reshape(count, 512), mask_s[:, at, :].reshape(count, 128), emb_ref[...])
    fb = fb_s[:, pl.ds(start // 8, cols // 8)].reshape(2, 1, cols, 512)
    fb = jnp.broadcast_to(fb, (2, 8, cols, 512)).reshape(count, 512)
    mixed = stream + mm(fine_s[:, at, :].reshape(count, 512), wo) + fb
    nm = normalize(mixed).astype(BF16)
    acc = mixed
    ahead = mm(nm, w1_s[:, :512])
    for f in range(4):
        now = ahead
        if f < 3:
            ahead = mm(nm, w1_s[:, 512 * f + 512 : 512 * f + 1024])
        acc = acc + mm(gelu(now), w2_s[512 * f : 512 * f + 512, :])
    out_s[:, at, :] = acc.astype(BF16).reshape(16, cols, 512)


LEFT, RIGHT, REST = pl.ds(0, 16), pl.ds(144, 16), pl.ds(160, 16)
N_COPIES = 42
QUERY, KEY, VALUE, OUT, CQUERY, CKEY, CVALUE, COUT = range(8)


def layer(
    tok_ref, mask_ref, emb_ref, wq_ref, wk_ref, wv_ref, wo_ref, cwq_ref, cwk_ref, cwv_ref, cwo_ref,
    w1_ref, w2_ref, ones_ref, qt_ref, kt_ref, scale_ref, cscale_ref, out_ref,
    tok_s, mask_s, w_s, w1_s, w2_s, out_s, fine_s,
    buf, ls_s, rs_s, lr_s, rr_s, corner_s, up_buf, dn_buf, q_s, k_s, v_s, ku_s, vu_s, kd_s, vd_s, o_s, l_s, m_s,
    psum, cin_s, cq_s, x_s, ck_s, cv_s, qz_s, po_s, ps_s, rz_s, rst_s, fb_s, c_ref, cc_ref,
    send_sem, recv_sem, load_sem, store_sem,
):
    t, r = lax.axis_index("tile"), lax.axis_index("region")
    prev, following = (t + 31) % 32, (t + 1) % 32
    left, right = (r + 3) % 4, (r + 1) % 4
    g, z_lo = t // 2, t % 2
    z_hi, core = r // 2, r % 2
    z = 2 * z_hi + z_lo

    def plane(step):
        return {"tile": 2 * ((g + step) % 16) + z_lo, "region": r}

    def column(step):
        other = (z + step) % 4
        return {"tile": 2 * g + other % 2, "region": 2 * (other // 2) + core}

    def copy(src, dst, index, where):
        return pltpu.make_async_remote_copy(
            src_ref=src, dst_ref=dst, send_sem=send_sem.at[index], recv_sem=recv_sem.at[index],
            device_id=where, device_id_type=MESH,
        )

    barrier = pltpu.get_barrier_semaphore()
    to_left, to_right = {"tile": t, "region": left}, {"tile": t, "region": right}
    for where in [to_left, to_right] + [{"tile": a, "region": b} for a in (prev, following) for b in (left, r, right)]:
        pl.semaphore_signal(barrier, inc=1, device_id=where, device_id_type=MESH)

    @pl.loop(1, 16)
    def _(step):
        pl.semaphore_signal(barrier, inc=1, device_id=plane(step), device_id_type=MESH)

    for step in (1, 2, 3):
        pl.semaphore_signal(barrier, inc=1, device_id=column(step), device_id_type=MESH)

    load_tok = pltpu.make_async_copy(tok_ref, tok_s, load_sem.at[0])
    load_tok.start()
    names = (wq_ref, wk_ref, wv_ref, wo_ref, cwq_ref, cwk_ref, cwv_ref, cwo_ref)
    loads = [pltpu.make_async_copy(ref, w_s.at[i], load_sem.at[1 + i]) for i, ref in enumerate(names)]
    load_1 = pltpu.make_async_copy(w1_ref, w1_s, load_sem.at[9])
    load_2 = pltpu.make_async_copy(w2_ref, w2_s, load_sem.at[10])
    for i in (CQUERY, QUERY, KEY, VALUE, CKEY, CVALUE, OUT, COUT):
        loads[i].start()
    load_1.start()
    load_2.start()

    ones = ones_ref[...]
    for h in range(HEADS):
        c_ref[h] = scale_ref[h] * FACTOR
        cc_ref[h] = cscale_ref[h] * FACTOR
    psum[...] = jnp.zeros_like(psum)
    up_buf[0] = jnp.zeros((176, 512), BF16)
    dn_buf[7] = jnp.zeros((176, 512), BF16)
    up_buf[:, REST, :] = jnp.zeros((8, 16, 512), BF16)
    dn_buf[:, REST, :] = jnp.zeros((8, 16, 512), BF16)
    load_tok.wait()

    def norm_rows(i):
        lo, hi = [], []
        total = jnp.zeros((128, 512), F32)
        for k in range(4):
            row = 4 * i + k
            m = jnp.broadcast_to(mask_ref[pl.ds(row, 1), :].astype(F32), (128, 128)).T.astype(BF16)
            mask_s[row] = m
            n = normalize(stream_of(tok_s[row], m, emb_ref[...]))
            nb = n.astype(BF16)
            buf[row] = nb
            total = total + nb.astype(F32)
            lo.append(n[:8])
            hi.append(n[120:])
        psum[i // 2] += total
        at = pl.ds(pl.multiple_of(32 * i, 32), 32)
        ls_s[at, :] = jnp.concatenate(lo, axis=0).astype(BF16)
        rs_s[at, :] = jnp.concatenate(hi, axis=0).astype(BF16)

    sides = [copy(ls_s, rr_s, 0, to_left), copy(rs_s, lr_s, 1, to_right)]
    first, last = pl.ds(0, 64), pl.ds(64, 64)
    corners = [
        copy(rs_s.at[first, :], corner_s.at[0], 2, {"tile": prev, "region": right}),
        copy(rs_s.at[last, :], corner_s.at[1], 3, {"tile": following, "region": right}),
        copy(ls_s.at[first, :], corner_s.at[2], 4, {"tile": prev, "region": left}),
        copy(ls_s.at[last, :], corner_s.at[3], 5, {"tile": following, "region": left}),
    ]

    def row_piece(k):
        src = pl.ds(pl.multiple_of(32 * k, 16), 32)
        dst = pl.ds(pl.multiple_of(16 + 32 * k, 16), 32)
        return (
            copy(buf.at[pl.ds(0, 7), src, :], dn_buf.at[pl.ds(0, 7), dst, :], 6 + k, {"tile": prev, "region": r}),
            copy(buf.at[pl.ds(9, 7), src, :], up_buf.at[pl.ds(1, 7), dst, :], 10 + k, {"tile": following, "region": r}),
        )

    @pl.loop(0, 4)
    def _(i):
        norm_rows(i)

    cin = normalize(jnp.sum(psum[...].reshape(32, 8, 512), axis=1) * (1.0 / 64.0)).astype(BF16)
    cin_s[...] = cin
    x_s[core, g] = cin
    loads[CQUERY].wait()
    cq = head_norm(mm(cin, w_s[CQUERY]), ones)
    cq_s[...] = cq
    qz_s[z] = cq
    loads[QUERY].wait()

    @pl.loop(0, 4)
    def _(i):
        rows = pl.ds(4 * i, 4)
        q_s[rows] = head_norm(mm(buf[rows].reshape(512, 512), w_s[QUERY]), ones).reshape(4, 128, 512)

    loads[KEY].wait()
    loads[VALUE].wait()

    def own_keys(i):
        rows = pl.ds(4 * i, 4)
        side = jnp.zeros((4, 8, 512), F32)
        n = jnp.concatenate([side, buf[rows].astype(F32), side], axis=1).astype(BF16)
        keys, vals = project(n.reshape(576, 512), w_s[KEY], w_s[VALUE], ones)
        k_s[rows] = keys.reshape(4, 144, 512)
        v_s[rows] = vals.reshape(4, 144, 512)

    @pl.loop(0, 2)
    def _(i):
        own_keys(i)

    def gather(step):
        return copy(cin_s, x_s.at[core, g], 13 + step, plane(step))

    asks = [copy(cq_s, qz_s.at[z], 28 + step, column(step)) for step in (1, 2, 3)]
    pl.semaphore_wait(barrier, 26)
    for c in sides:
        c.start()

    @pl.loop(1, 16)
    def _(step):
        gather(step).start()

    for c in asks:
        c.start()
    for c in row_piece(0):
        c.start()

    @pl.loop(2, 4)
    def _(i):
        own_keys(i)

    def attend_pair(first, second):
        for p in range(8):
            attend_own((first, second)[p // 4], p % 4, q_s, k_s, v_s, qt_ref, kt_ref, c_ref, o_s, l_s, m_s)

    @pl.loop(0, 3)
    def _(j):
        attend_pair(2 * j + 1, 2 * j + 2)

    for c in row_piece(1):
        c.start()
    for c in corners[:2]:
        c.start()

    @pl.loop(1, 16)
    def _(step):
        gather(step).wait_recv()

    sibling = copy(x_s.at[core], x_s.at[core], 32, {"tile": t, "region": 2 * z_hi + 1 - core})
    sibling.start()
    replies = []
    for step in (1, 2, 3):
        rows = pl.ds(pl.multiple_of(32 * ((z + step) % 4), 32), 32)
        replies.append(copy(po_s.at[rows, :], rz_s.at[z], 32 + step, column(step)))
        replies.append(copy(ps_s.at[:, rows, :], rst_s.at[z], 35 + step, column(step)))

    for c in sides:
        c.wait_recv()
    edges = [
        lr_s[...].astype(F32).reshape(16, 8, 512),
        buf[:, 0:16, :].astype(F32)[:, :8],
        buf[:, 112:128, :].astype(F32)[:, 8:],
        rr_s[...].astype(F32).reshape(16, 8, 512),
    ]
    n = [jnp.concatenate(edges[i : i + 2], axis=1).astype(BF16).reshape(256, 512) for i in (0, 2)]
    keys, vals = project(jnp.concatenate(n, axis=0), w_s[KEY], w_s[VALUE], ones)
    for i, cols in ((0, pl.ds(0, 16)), (1, pl.ds(128, 16))):
        part = slice(256 * i, 256 * i + 256)
        k_s[:, cols, :] = keys[part].reshape(16, 16, 512)
        v_s[:, cols, :] = vals[part].reshape(16, 16, 512)
    attend_pair(0, 7)

    sibling.wait_recv()
    for c in asks:
        c.wait_recv()
    loads[CKEY].wait()
    loads[CVALUE].wait()
    coarse_part(x_s, qz_s, w_s, cc_ref, ones, ck_s, cv_s, po_s, ps_s)
    for c in replies:
        c.start()
    mine = pl.ds(pl.multiple_of(32 * z, 32), 32)
    rz_s[z] = po_s[mine, :]
    rst_s[z] = ps_s[:, mine, :]
    for c in row_piece(0):
        c.wait_send()
    for c in row_piece(2):
        c.start()

    def place(source, dst, where):
        x = source.astype(F32).reshape(8, 8, 512)
        zero = jnp.zeros_like(x)
        both = [zero, x] if where is LEFT else [x, zero]
        dst[:, where, :] = jnp.concatenate(both, axis=1).astype(BF16)

    def attend(j):
        fine = [
            attend_all(j, p, q_s, ku_s, kd_s, vu_s, vd_s, qt_ref, kt_ref, c_ref, o_s, l_s, m_s)
            for p in range(4)
        ]
        at = pl.ds(pl.multiple_of(16 * j, 16), 16)
        fine_s[:, at, :] = jnp.concatenate(fine, axis=1).reshape(16, 16, 512)

    def store(start, cols, index):
        at = pl.ds(pl.multiple_of(start, 16), cols)
        return pltpu.make_async_copy(out_s.at[:, at, :], out_ref.at[:, at, :], store_sem.at[index])

    def close(start, cols, index):
        finish(start, cols, fine_s, tok_s, mask_s, emb_ref, fb_s, w_s[OUT], w1_s, w2_s, out_s)
        store(start, cols, index).start()

    @pl.loop(0, 5)
    def _(i):
        @pl.when(i < 4)
        def _():
            for c in row_piece(i):
                c.wait_recv()

        @pl.when(i == 0)
        def _():
            for c in corners[:2]:
                c.wait_recv()
            place(corner_s[0], dn_buf, LEFT)
            place(corner_s[1], up_buf, LEFT)

        @pl.when(i == 4)
        def _():
            for c in corners[2:]:
                c.wait_recv()
            place(corner_s[2], dn_buf, RIGHT)
            place(corner_s[3], up_buf, RIGHT)

        src = pl.ds(pl.multiple_of(32 * i, 32), 48)
        cols = pl.ds(pl.multiple_of(32 * i, 32), 32)
        n = jnp.concatenate([b[:, src, :].astype(F32)[:, 8:40].astype(BF16) for b in (up_buf, dn_buf)], axis=0)
        keys, vals = project(n.reshape(512, 512), w_s[KEY], w_s[VALUE], ones)
        keys, vals = keys.reshape(16, 32, 512), vals.reshape(16, 32, 512)
        ku_s[:, cols, :], kd_s[:, cols, :] = keys[:8], keys[8:]
        vu_s[:, cols, :], vd_s[:, cols, :] = vals[:8], vals[8:]

        @pl.when(i == 0)
        def _():
            attend(0)
            for c in replies:
                c.wait_recv()
            loads[COUT].wait()
            feedback = mm(coarse_join(rz_s, rst_s), w_s[COUT])
            fb_s[...] = jnp.broadcast_to(feedback.reshape(32, 1, 512), (32, 8, 512)).reshape(2, 16, 8, 512)
            loads[OUT].wait()
            load_1.wait()
            load_2.wait()
            close(0, 16, 0)

        @pl.when(i == 1)
        def _():
            for c in row_piece(1):
                c.wait_send()
            for c in row_piece(3) + tuple(corners[2:]):
                c.start()

        @pl.when((i > 0) & (i < 4))
        def _():
            attend(2 * i - 1)
            attend(2 * i)
            close(32 * i - 16, 32, i)

        @pl.when(i == 4)
        def _():
            attend(7)
            close(112, 16, 4)

    store(0, 16, 0).wait()

    @pl.loop(1, 4)
    def _(i):
        store(32 * i - 16, 32, i).wait()

    store(112, 16, 4).wait()
    for c in sides + corners + asks + [sibling] + replies:
        c.wait_send()

    for k in (2, 3):
        for c in row_piece(k):
            c.wait_send()

    @pl.loop(1, 16)
    def _(step):
        gather(step).wait_send()


def coarse_part(x_s, qz_s, w_s, cc_ref, ones, ck_s, cv_s, po_s, ps_s):
    @pl.loop(0, 2)
    def _(i):
        x = x_s[i].reshape(512, 512)
        rows = pl.ds(pl.multiple_of(512 * i, 512), 512)
        k, v = project(x, w_s[CKEY], w_s[CVALUE], ones)
        ck_s[rows, :] = k
        cv_s[rows, :] = v

    q = qz_s[...].reshape(128, 512)
    lane = lax.broadcasted_iota(jnp.int32, (128, 128), 1)
    head = lax.broadcasted_iota(jnp.int32, (128, 256), 1) // 64
    tops = jnp.zeros((128, 128), F32)
    sums = jnp.zeros((128, 128), F32)
    for half in range(2):
        lanes = slice(256 * half, 256 * half + 256)
        qh = q[:, lanes]
        rows = jnp.concatenate([jnp.where(head == h, qh, jnp.zeros_like(qh)) for h in range(4)], axis=0)
        s = lax.dot_general(rows, ck_s[:, lanes], NT, preferred_element_type=F32)
        weights = []
        for h in range(4):
            c = cc_ref[4 * half + h]
            part = s[128 * h : 128 * h + 128]
            top = jnp.max(part, axis=-1, keepdims=True)
            w = jnp.exp2((part - top) * c)
            tops = jnp.where(lane == 4 * half + h, top * c, tops)
            sums = jnp.where(lane == 4 * half + h, jnp.sum(w, axis=-1, keepdims=True), sums)
            weights.append(w.astype(BF16))
        o = mm(jnp.concatenate(weights, axis=0), cv_s[:, lanes])
        picked = o[:128]
        for h in range(1, 4):
            picked = jnp.where(head == h, o[128 * h : 128 * h + 128], picked)
        po_s[:, lanes] = picked
    ps_s[0] = tops
    ps_s[1] = sums


def coarse_join(rz_s, rs_s):
    top = jnp.maximum(jnp.maximum(rs_s[0, 0], rs_s[1, 0]), jnp.maximum(rs_s[2, 0], rs_s[3, 0]))
    scale = [jnp.exp2(rs_s[i, 0] - top) for i in range(4)]
    total = sum(scale[i] * rs_s[i, 1] for i in range(4))
    low = lax.broadcasted_iota(jnp.int32, (32, 128), 1) < 64
    joined = jnp.zeros((32, 512), F32)
    for i in range(4):
        a = scale[i] / total
        wide = [
            jnp.where(low, jnp.broadcast_to(a[:, 2 * p : 2 * p + 1], (32, 128)), jnp.broadcast_to(a[:, 2 * p + 1 : 2 * p + 2], (32, 128)))
            for p in range(4)
        ]
        joined = joined + jnp.concatenate(wide, axis=1) * rz_s[i]
    return joined.astype(BF16)


def body(
    tokens, pore_mask, solid_embed, fine_query, fine_key, fine_value, fine_out, fine_scale,
    coarse_query, coarse_key, coarse_value, coarse_out, coarse_scale, mlp_in, mlp_out,
):
    vm = pl.BlockSpec(memory_space=pltpu.VMEM)
    sm = pl.BlockSpec(memory_space=pltpu.SMEM)
    hbm = pl.BlockSpec(memory_space=pl.ANY)

    def half(*shape):
        return pltpu.VMEM(shape, BF16)

    def full(*shape):
        return pltpu.VMEM(shape, F32)

    dma = pltpu.SemaphoreType.DMA
    return pl.pallas_call(
        layer,
        out_shape=jax.ShapeDtypeStruct((16, 128, 512), BF16),
        in_specs=[hbm, vm, vm] + [hbm] * 10 + [vm] * 3 + [sm] * 2,
        out_specs=hbm,
        scratch_shapes=[
            half(16, 128, 512),
            half(16, 128, 128),
            half(8, 512, 512),
            half(512, 2048),
            half(2048, 512),
            half(16, 128, 512),
            half(16, 128, 512),
            half(16, 128, 512),
            half(128, 512),
            half(128, 512),
            half(128, 512),
            half(128, 512),
            half(4, 64, 512),
            half(8, 176, 512),
            half(8, 176, 512),
            half(16, 128, 512),
            half(16, 144, 512),
            half(16, 144, 512),
            half(8, 160, 512),
            half(8, 160, 512),
            half(8, 160, 512),
            half(8, 160, 512),
            full(8, 4, 256, 128),
            full(8, 4, 256, 128),
            full(8, 4, 256, 128),
            full(2, 128, 512),
            half(32, 512),
            half(32, 512),
            half(2, 16, 32, 512),
            half(1024, 512),
            half(1024, 512),
            half(4, 32, 512),
            full(128, 512),
            full(2, 128, 128),
            full(4, 32, 512),
            full(4, 2, 32, 128),
            full(2, 16, 8, 512),
            pltpu.SMEM((8,), F32),
            pltpu.SMEM((8,), F32),
            dma((N_COPIES,)),
            dma((N_COPIES,)),
            dma((11,)),
            dma((5,)),
        ],
        compiler_params=pltpu.CompilerParams(
            collective_id=0, has_side_effects=True, vmem_limit_bytes=62 * 2**20
        ),
    )(
        tokens, pore_mask, solid_embed.reshape(1, 512), fine_query, fine_key, fine_value, fine_out,
        coarse_query, coarse_key, coarse_value, coarse_out, mlp_in, mlp_out,
        block_ones(), query_table(), key_tables(), fine_scale, coarse_scale,
    )


def solution(mesh):
    placed = (P("tile", "region", None), P("tile", "region")) + (P(),) * 13
    return jax.shard_map(
        body, mesh=mesh, in_specs=placed, out_specs=P("tile", "region", None), check_vma=False
    )
```

```python
import functools
import math

import jax
import jax.numpy as jnp
import numpy as np
from jax import lax
from jax.experimental import pallas as pl
from jax.experimental.pallas import tpu as pltpu
from jax.sharding import PartitionSpec as P

F32, BF16 = jnp.float32, jnp.bfloat16
MESH = pl.DeviceIdType.MESH
HEADS = 8
EPS = 1e-6
BIG = 131072.0
FACTOR = math.log2(math.e) / 8.0
TAIL = (
    -1.0002404059668364,
    -1.1475987944049173,
    -0.46737700467532134,
    -0.04592394901048988,
    0.005166375711832039,
    -0.00025544077122896525,
)
NT = (((1,), (1,)), ((), ()))


def mm(a, b):
    return jnp.dot(a, b, preferred_element_type=F32)


def gelu(x):
    x = x.astype(BF16)
    z = jnp.abs(x)
    p = z * BF16(TAIL[5]) + BF16(TAIL[4])
    for c in TAIL[3::-1]:
        p = p * z + BF16(c)
    return jnp.maximum(x, BF16(0)) - z * jnp.exp2(p)


def block_ones():
    i = np.arange(256) // 64
    return jnp.asarray((i[:, None] == i[None, :]).astype(np.float32) / 64.0, BF16)


def key_tables():
    t = np.zeros((4, 8, 32, 128), np.float32)
    q = np.arange(16)
    for chunk in range(4):
        for row in range(8):
            away = np.abs(q - (8 * (chunk - 1) + row))
            t[chunk, row, :, 0:16] = np.where(away <= 7, 0.0, -BIG)[None, :]
        for col in range(32):
            t[chunk, :, col, 16:32] = np.where(np.abs(q - (col - 8)) <= 7, 0.0, -BIG)[None, :]
    return jnp.asarray(t.reshape(4, 256, 128), BF16)


def query_table():
    t = np.zeros((16, 16, 128), np.float32)
    for i in range(16):
        t[i, :, i] = 1.0
        t[:, i, 16 + i] = 1.0
    return jnp.asarray(t.reshape(256, 128), BF16)


def head_norm(p, ones):
    sq = (p * p).astype(BF16)
    ms = jnp.concatenate([mm(sq[:, :256], ones), mm(sq[:, 256:], ones)], axis=1)
    return (p * lax.rsqrt(ms + EPS)).astype(BF16)


def normalize(x):
    return x * lax.rsqrt(jnp.mean(x * x, axis=-1, keepdims=True) + EPS)


def queries_of(q_s, qt_ref, j, p):
    q = q_s[:, pl.ds(pl.multiple_of(16 * j, 16), 16), 128 * p : 128 * p + 128].reshape(256, 128)
    low = lax.broadcasted_iota(jnp.int32, (256, 128), 1) < 64
    zero = jnp.zeros_like(q)
    qt = qt_ref[...]
    return [
        jnp.concatenate([jnp.where(low, q, zero), qt], axis=1),
        jnp.concatenate([jnp.where(low, zero, q), qt], axis=1),
    ]


def chunk_of(ref, row, j, p, extra):
    cols = pl.ds(pl.multiple_of(16 * j, 16), 32)
    x = ref[row : row + 8, cols, 128 * p : 128 * p + 128].reshape(256, 128)
    return jnp.concatenate([x, extra], axis=1)


def soft(s, c):
    top = jnp.max(s, axis=-1, keepdims=True)
    return jnp.exp2((s - top) * c).astype(BF16), top * c


def merge(first, second):
    low = lax.broadcasted_iota(jnp.int32, first.shape, 1) < 64
    return jnp.where(low, first, second)


def attend_own(j, p, q_s, k_s, v_s, qt_ref, kt_ref, c_ref, o_s, l_s, m_s):
    qa, qb = queries_of(q_s, qt_ref, j, p)
    ones = jnp.ones((256, 128), BF16)
    keys = jnp.concatenate([chunk_of(k_s, 8 * i, j, p, kt_ref[1 + i]) for i in range(2)], axis=0)
    vals = jnp.concatenate([chunk_of(v_s, 8 * i, j, p, ones) for i in range(2)], axis=0)
    s = lax.dot_general(jnp.concatenate([qa, qb], axis=0), keys, NT, preferred_element_type=F32)
    wa, ma = soft(s[:256], c_ref[2 * p])
    wb, mb = soft(s[256:], c_ref[2 * p + 1])
    o = mm(jnp.concatenate([wa, wb], axis=0), vals)
    o_s[j, p] = merge(o[:256, :128], o[256:, :128])
    l_s[j, p] = merge(o[:256, 128:], o[256:, 128:])
    m_s[j, p] = merge(jnp.broadcast_to(ma, (256, 128)), jnp.broadcast_to(mb, (256, 128)))


def attend_all(j, p, q_s, ku_s, kd_s, vu_s, vd_s, qt_ref, kt_ref, c_ref, o_s, l_s, m_s):
    qa, qb = queries_of(q_s, qt_ref, j, p)
    ones = jnp.ones((256, 128), BF16)
    done = []
    for k_s, v_s, table, part in ((ku_s, vu_s, 0, slice(0, 128)), (kd_s, vd_s, 3, slice(128, 256))):
        keys = chunk_of(k_s, 0, j, p, kt_ref[table])
        vals = chunk_of(v_s, 0, j, p, ones)
        q = jnp.concatenate([qa[part], qb[part]], axis=0)
        s = lax.dot_general(q, keys, NT, preferred_element_type=F32)
        wa, ma = soft(s[:128], c_ref[2 * p])
        wb, mb = soft(s[128:], c_ref[2 * p + 1])
        o = mm(jnp.concatenate([wa, wb], axis=0), vals)
        o2 = merge(o[:128, :128], o[128:, :128])
        l2 = merge(o[:128, 128:], o[128:, 128:])
        m2 = merge(jnp.broadcast_to(ma, (128, 128)), jnp.broadcast_to(mb, (128, 128)))
        o1, l1, m1 = o_s[j, p, part], l_s[j, p, part], m_s[j, p, part]
        top = jnp.maximum(m1, m2)
        a1, a2 = jnp.exp2(m1 - top), jnp.exp2(m2 - top)
        done.append(((o1 * a1 + o2 * a2) / (l1 * a1 + l2 * a2)).astype(BF16))
    return jnp.concatenate(done, axis=0)


def project(n, wk, wv, ones):
    return head_norm(mm(n, wk), ones), mm(n, wv).astype(BF16)


def stream_of(tok, mask, emb):
    m = mask.astype(F32)
    return tok.astype(F32) + jnp.concatenate([m] * 4, axis=1) * emb


def finish(start, cols, fine_s, tok_s, mask_s, emb_ref, fb_s, wo, w1_s, w2_s, out_s):
    count = 16 * cols
    at = pl.ds(pl.multiple_of(start, 16), cols)
    stream = stream_of(tok_s[:, at, :].reshape(count, 512), mask_s[:, at, :].reshape(count, 128), emb_ref[...])
    fb = fb_s[:, pl.ds(start // 8, cols // 8)].reshape(2, 1, cols, 512)
    fb = jnp.broadcast_to(fb, (2, 8, cols, 512)).reshape(count, 512)
    mixed = stream + mm(fine_s[:, at, :].reshape(count, 512), wo) + fb
    nm = normalize(mixed).astype(BF16)
    acc = mixed
    ahead = mm(nm, w1_s[:, :512])
    for f in range(4):
        now = ahead
        if f < 3:
            ahead = mm(nm, w1_s[:, 512 * f + 512 : 512 * f + 1024])
        acc = acc + mm(gelu(now), w2_s[512 * f : 512 * f + 512, :])
    out_s[:, at, :] = acc.astype(BF16).reshape(16, cols, 512)


LEFT, RIGHT, REST = pl.ds(0, 16), pl.ds(144, 16), pl.ds(160, 16)
N_COPIES = 42
QUERY, KEY, VALUE, OUT, CQUERY, CKEY, CVALUE, COUT = range(8)


def layer(
    tok_ref, mask_ref, emb_ref, wq_ref, wk_ref, wv_ref, wo_ref, cwq_ref, cwk_ref, cwv_ref, cwo_ref,
    w1_ref, w2_ref, ones_ref, qt_ref, kt_ref, scale_ref, cscale_ref, out_ref,
    tok_s, mask_s, w_s, w1_s, w2_s, out_s, fine_s,
    buf, ls_s, rs_s, lr_s, rr_s, corner_s, up_buf, dn_buf, q_s, k_s, v_s, ku_s, vu_s, kd_s, vd_s, o_s, l_s, m_s,
    psum, cin_s, cq_s, x_s, ck_s, cv_s, qz_s, po_s, ps_s, rz_s, rst_s, fb_s, c_ref, cc_ref,
    send_sem, recv_sem, load_sem, store_sem,
):
    t, r = lax.axis_index("tile"), lax.axis_index("region")
    prev, following = (t + 31) % 32, (t + 1) % 32
    left, right = (r + 3) % 4, (r + 1) % 4
    g, z_lo = t // 2, t % 2
    z_hi, core = r // 2, r % 2
    z = 2 * z_hi + z_lo

    def plane(step):
        return {"tile": 2 * ((g + step) % 16) + z_lo, "region": r}

    def column(step):
        other = (z + step) % 4
        return {"tile": 2 * g + other % 2, "region": 2 * (other // 2) + core}

    def copy(src, dst, index, where):
        return pltpu.make_async_remote_copy(
            src_ref=src, dst_ref=dst, send_sem=send_sem.at[index], recv_sem=recv_sem.at[index],
            device_id=where, device_id_type=MESH,
        )

    barrier = pltpu.get_barrier_semaphore()
    to_left, to_right = {"tile": t, "region": left}, {"tile": t, "region": right}
    for where in [to_left, to_right] + [{"tile": a, "region": b} for a in (prev, following) for b in (left, r, right)]:
        pl.semaphore_signal(barrier, inc=1, device_id=where, device_id_type=MESH)

    @pl.loop(1, 16)
    def _(step):
        pl.semaphore_signal(barrier, inc=1, device_id=plane(step), device_id_type=MESH)

    for step in (1, 2, 3):
        pl.semaphore_signal(barrier, inc=1, device_id=column(step), device_id_type=MESH)

    load_tok = pltpu.make_async_copy(tok_ref, tok_s, load_sem.at[0])
    load_tok.start()
    names = (wq_ref, wk_ref, wv_ref, wo_ref, cwq_ref, cwk_ref, cwv_ref, cwo_ref)
    loads = [pltpu.make_async_copy(ref, w_s.at[i], load_sem.at[1 + i]) for i, ref in enumerate(names)]
    load_1 = pltpu.make_async_copy(w1_ref, w1_s, load_sem.at[9])
    load_2 = pltpu.make_async_copy(w2_ref, w2_s, load_sem.at[10])
    for i in (CQUERY, QUERY, KEY, VALUE, CKEY, CVALUE, OUT, COUT):
        loads[i].start()
    load_1.start()
    load_2.start()

    ones = ones_ref[...]
    for h in range(HEADS):
        c_ref[h] = scale_ref[h] * FACTOR
        cc_ref[h] = cscale_ref[h] * FACTOR
    psum[...] = jnp.zeros_like(psum)
    up_buf[0] = jnp.zeros((176, 512), BF16)
    dn_buf[7] = jnp.zeros((176, 512), BF16)
    up_buf[:, REST, :] = jnp.zeros((8, 16, 512), BF16)
    dn_buf[:, REST, :] = jnp.zeros((8, 16, 512), BF16)
    load_tok.wait()

    def norm_rows(i):
        lo, hi = [], []
        total = jnp.zeros((128, 512), F32)
        for k in range(4):
            row = 4 * i + k
            m = jnp.broadcast_to(mask_ref[pl.ds(row, 1), :].astype(F32), (128, 128)).T.astype(BF16)
            mask_s[row] = m
            n = normalize(stream_of(tok_s[row], m, emb_ref[...]))
            nb = n.astype(BF16)
            buf[row] = nb
            total = total + nb.astype(F32)
            lo.append(n[:8])
            hi.append(n[120:])
        psum[i // 2] += total
        at = pl.ds(pl.multiple_of(32 * i, 32), 32)
        ls_s[at, :] = jnp.concatenate(lo, axis=0).astype(BF16)
        rs_s[at, :] = jnp.concatenate(hi, axis=0).astype(BF16)

    sides = [copy(ls_s, rr_s, 0, to_left), copy(rs_s, lr_s, 1, to_right)]
    first, last = pl.ds(0, 64), pl.ds(64, 64)
    corners = [
        copy(rs_s.at[first, :], corner_s.at[0], 2, {"tile": prev, "region": right}),
        copy(rs_s.at[last, :], corner_s.at[1], 3, {"tile": following, "region": right}),
        copy(ls_s.at[first, :], corner_s.at[2], 4, {"tile": prev, "region": left}),
        copy(ls_s.at[last, :], corner_s.at[3], 5, {"tile": following, "region": left}),
    ]

    def row_part(start, cols, up, down):
        src = pl.ds(pl.multiple_of(start, 16), cols)
        dst = pl.ds(pl.multiple_of(16 + start, 16), cols)
        return (
            copy(buf.at[pl.ds(0, 7), src, :], dn_buf.at[pl.ds(0, 7), dst, :], up, {"tile": prev, "region": r}),
            copy(buf.at[pl.ds(9, 7), src, :], up_buf.at[pl.ds(1, 7), dst, :], down, {"tile": following, "region": r}),
        )

    def row_piece(k):
        return row_part(32 * k, 32, 6 + k, 10 + k)

    late = row_part(96, 16, 9, 13)
    latest = row_part(112, 16, 39, 40)

    @pl.loop(0, 4)
    def _(i):
        norm_rows(i)

    cin = normalize(jnp.sum(psum[...].reshape(32, 8, 512), axis=1) * (1.0 / 64.0)).astype(BF16)
    cin_s[...] = cin
    x_s[core, g] = cin
    loads[CQUERY].wait()
    cq = head_norm(mm(cin, w_s[CQUERY]), ones)
    cq_s[...] = cq
    qz_s[z] = cq
    loads[QUERY].wait()

    @pl.loop(0, 4)
    def _(i):
        rows = pl.ds(4 * i, 4)
        q_s[rows] = head_norm(mm(buf[rows].reshape(512, 512), w_s[QUERY]), ones).reshape(4, 128, 512)

    loads[KEY].wait()
    loads[VALUE].wait()

    def own_keys(i):
        rows = pl.ds(4 * i, 4)
        side = jnp.zeros((4, 8, 512), F32)
        n = jnp.concatenate([side, buf[rows].astype(F32), side], axis=1).astype(BF16)
        keys, vals = project(n.reshape(576, 512), w_s[KEY], w_s[VALUE], ones)
        k_s[rows] = keys.reshape(4, 144, 512)
        v_s[rows] = vals.reshape(4, 144, 512)

    @pl.loop(0, 2)
    def _(i):
        own_keys(i)

    def gather(step):
        return copy(cin_s, x_s.at[core, g], 13 + step, plane(step))

    asks = [copy(cq_s, qz_s.at[z], 28 + step, column(step)) for step in (1, 2, 3)]
    pl.semaphore_wait(barrier, 26)
    for c in sides:
        c.start()

    @pl.loop(1, 16)
    def _(step):
        gather(step).start()

    for c in asks:
        c.start()
    for c in row_piece(0):
        c.start()

    @pl.loop(2, 4)
    def _(i):
        own_keys(i)

    def attend_pair(first, second):
        for p in range(8):
            attend_own((first, second)[p // 4], p % 4, q_s, k_s, v_s, qt_ref, kt_ref, c_ref, o_s, l_s, m_s)

    @pl.loop(0, 3)
    def _(j):
        attend_pair(2 * j + 1, 2 * j + 2)

    for c in row_piece(1):
        c.start()
    for c in corners[:2]:
        c.start()

    @pl.loop(1, 16)
    def _(step):
        gather(step).wait_recv()

    sibling = copy(x_s.at[core], x_s.at[core], 32, {"tile": t, "region": 2 * z_hi + 1 - core})
    sibling.start()
    replies = []
    for step in (1, 2, 3):
        rows = pl.ds(pl.multiple_of(32 * ((z + step) % 4), 32), 32)
        replies.append(copy(po_s.at[rows, :], rz_s.at[z], 32 + step, column(step)))
        replies.append(copy(ps_s.at[rows, :], rst_s.at[z], 35 + step, column(step)))

    for c in sides:
        c.wait_recv()
    edges = [
        lr_s[...].astype(F32).reshape(16, 8, 512),
        buf[:, 0:16, :].astype(F32)[:, :8],
        buf[:, 112:128, :].astype(F32)[:, 8:],
        rr_s[...].astype(F32).reshape(16, 8, 512),
    ]
    n = [jnp.concatenate(edges[i : i + 2], axis=1).astype(BF16).reshape(256, 512) for i in (0, 2)]
    keys, vals = project(jnp.concatenate(n, axis=0), w_s[KEY], w_s[VALUE], ones)
    for i, cols in ((0, pl.ds(0, 16)), (1, pl.ds(128, 16))):
        part = slice(256 * i, 256 * i + 256)
        k_s[:, cols, :] = keys[part].reshape(16, 16, 512)
        v_s[:, cols, :] = vals[part].reshape(16, 16, 512)
    attend_pair(0, 7)

    sibling.wait_recv()
    for c in asks:
        c.wait_recv()
    loads[CKEY].wait()
    loads[CVALUE].wait()
    coarse_part(x_s, qz_s, w_s, cc_ref, ones, ck_s, cv_s, po_s, ps_s)
    for c in replies:
        c.start()
    mine = pl.ds(pl.multiple_of(32 * z, 32), 32)
    rz_s[z] = po_s[mine, :]
    rst_s[z] = ps_s[mine, :]
    for c in row_piece(0):
        c.wait_send()
    for c in row_piece(2):
        c.start()

    def place(source, dst, where):
        x = source.astype(F32).reshape(8, 8, 512)
        zero = jnp.zeros_like(x)
        both = [zero, x] if where is LEFT else [x, zero]
        dst[:, where, :] = jnp.concatenate(both, axis=1).astype(BF16)

    def attend(j):
        fine = [
            attend_all(j, p, q_s, ku_s, kd_s, vu_s, vd_s, qt_ref, kt_ref, c_ref, o_s, l_s, m_s)
            for p in range(4)
        ]
        at = pl.ds(pl.multiple_of(16 * j, 16), 16)
        fine_s[:, at, :] = jnp.concatenate(fine, axis=1).reshape(16, 16, 512)

    def store(start, cols, index):
        at = pl.ds(pl.multiple_of(start, 16), cols)
        return pltpu.make_async_copy(out_s.at[:, at, :], out_ref.at[:, at, :], store_sem.at[index])

    def close(start, cols, index):
        finish(start, cols, fine_s, tok_s, mask_s, emb_ref, fb_s, w_s[OUT], w1_s, w2_s, out_s)
        store(start, cols, index).start()

    def halo(start, width):
        src = pl.ds(pl.multiple_of(start, 16), width + 16)
        cols = pl.ds(pl.multiple_of(start, 16), width)
        n = [b[:, src, :].astype(F32)[:, 8 : width + 8].astype(BF16) for b in (up_buf, dn_buf)]
        n = jnp.concatenate(n, axis=0).reshape(16 * width, 512)
        keys, vals = project(n, w_s[KEY], w_s[VALUE], ones)
        keys, vals = keys.reshape(16, width, 512), vals.reshape(16, width, 512)
        ku_s[:, cols, :], kd_s[:, cols, :] = keys[:8], keys[8:]
        vu_s[:, cols, :], vd_s[:, cols, :] = vals[:8], vals[8:]

    @pl.loop(0, 3)
    def _(i):
        for c in row_piece(i):
            c.wait_recv()

        @pl.when(i == 0)
        def _():
            for c in corners[:2]:
                c.wait_recv()
            place(corner_s[0], dn_buf, LEFT)
            place(corner_s[1], up_buf, LEFT)

        halo(32 * i, 32)

        @pl.when(i == 0)
        def _():
            attend(0)
            for c in replies:
                c.wait_recv()
            loads[COUT].wait()
            feedback = mm(coarse_join(rz_s, rst_s), w_s[COUT])
            fb_s[...] = jnp.broadcast_to(feedback.reshape(32, 1, 512), (32, 8, 512)).reshape(2, 16, 8, 512)
            loads[OUT].wait()
            load_1.wait()
            load_2.wait()
            close(0, 16, 0)

        @pl.when(i == 1)
        def _():
            for c in row_piece(1):
                c.wait_send()
            for c in late + tuple(corners[2:]) + latest:
                c.start()

        @pl.when(i > 0)
        def _():
            attend(2 * i - 1)
            attend(2 * i)
            close(32 * i - 16, 32, i)

    for c in late:
        c.wait_recv()
    halo(96, 16)
    attend(5)
    close(80, 16, 3)
    for c in latest + tuple(corners[2:]):
        c.wait_recv()
    place(corner_s[2], dn_buf, RIGHT)
    place(corner_s[3], up_buf, RIGHT)
    halo(112, 32)
    attend(6)
    attend(7)
    close(96, 32, 4)

    store(0, 16, 0).wait()

    store(16, 32, 1).wait()
    store(48, 32, 2).wait()
    store(80, 16, 3).wait()
    store(96, 32, 4).wait()
    for c in sides + corners + asks + [sibling] + replies:
        c.wait_send()

    for c in row_piece(2) + late + latest:
        c.wait_send()

    @pl.loop(1, 16)
    def _(step):
        gather(step).wait_send()


def coarse_part(x_s, qz_s, w_s, cc_ref, ones, ck_s, cv_s, po_s, ps_s):
    @pl.loop(0, 2)
    def _(i):
        x = x_s[i].reshape(512, 512)
        rows = pl.ds(pl.multiple_of(512 * i, 512), 512)
        k, v = project(x, w_s[CKEY], w_s[CVALUE], ones)
        ck_s[rows, :] = k
        cv_s[rows, :] = v

    q = qz_s[...].reshape(128, 512)
    lane = lax.broadcasted_iota(jnp.int32, (128, 128), 1)
    head = lax.broadcasted_iota(jnp.int32, (128, 256), 1) // 64
    tops = jnp.zeros((128, 128), F32)
    for half in range(2):
        lanes = slice(256 * half, 256 * half + 256)
        qh = q[:, lanes]
        rows = jnp.concatenate([jnp.where(head == h, qh, jnp.zeros_like(qh)) for h in range(4)], axis=0)
        s = lax.dot_general(rows, ck_s[:, lanes], NT, preferred_element_type=F32)
        weights, totals = [], []
        for h in range(4):
            c = cc_ref[4 * half + h]
            part = s[128 * h : 128 * h + 128]
            top = jnp.max(part, axis=-1, keepdims=True)
            w = jnp.exp2((part - top) * c)
            total = jnp.sum(w, axis=-1, keepdims=True)
            tops = jnp.where(lane == 4 * half + h, top * c + jnp.log2(total), tops)
            totals.append(total)
            weights.append(w.astype(BF16))
        o = mm(jnp.concatenate(weights, axis=0), cv_s[:, lanes])
        picked = o[:128] / totals[0]
        for h in range(1, 4):
            picked = jnp.where(head == h, o[128 * h : 128 * h + 128] / totals[h], picked)
        po_s[:, lanes] = picked.astype(BF16)
    ps_s[...] = tops


def coarse_join(rz_s, rs_s):
    top = jnp.maximum(jnp.maximum(rs_s[0], rs_s[1]), jnp.maximum(rs_s[2], rs_s[3]))
    scale = [jnp.exp2(rs_s[i] - top) for i in range(4)]
    total = sum(scale)
    low = lax.broadcasted_iota(jnp.int32, (32, 128), 1) < 64
    joined = jnp.zeros((32, 512), F32)
    for i in range(4):
        a = scale[i] / total
        wide = [
            jnp.where(low, jnp.broadcast_to(a[:, 2 * p : 2 * p + 1], (32, 128)), jnp.broadcast_to(a[:, 2 * p + 1 : 2 * p + 2], (32, 128)))
            for p in range(4)
        ]
        joined = joined + jnp.concatenate(wide, axis=1) * rz_s[i].astype(F32)
    return joined.astype(BF16)


def body(
    tokens, pore_mask, solid_embed, fine_query, fine_key, fine_value, fine_out, fine_scale,
    coarse_query, coarse_key, coarse_value, coarse_out, coarse_scale, mlp_in, mlp_out,
):
    vm = pl.BlockSpec(memory_space=pltpu.VMEM)
    sm = pl.BlockSpec(memory_space=pltpu.SMEM)
    hbm = pl.BlockSpec(memory_space=pl.ANY)

    def half(*shape):
        return pltpu.VMEM(shape, BF16)

    def full(*shape):
        return pltpu.VMEM(shape, F32)

    dma = pltpu.SemaphoreType.DMA
    return pl.pallas_call(
        layer,
        out_shape=jax.ShapeDtypeStruct((16, 128, 512), BF16),
        in_specs=[hbm, vm, vm] + [hbm] * 10 + [vm] * 3 + [sm] * 2,
        out_specs=hbm,
        scratch_shapes=[
            half(16, 128, 512),
            half(16, 128, 128),
            half(8, 512, 512),
            half(512, 2048),
            half(2048, 512),
            half(16, 128, 512),
            half(16, 128, 512),
            half(16, 128, 512),
            half(128, 512),
            half(128, 512),
            half(128, 512),
            half(128, 512),
            half(4, 64, 512),
            half(8, 176, 512),
            half(8, 176, 512),
            half(16, 128, 512),
            half(16, 144, 512),
            half(16, 144, 512),
            half(8, 160, 512),
            half(8, 160, 512),
            half(8, 160, 512),
            half(8, 160, 512),
            full(8, 4, 256, 128),
            full(8, 4, 256, 128),
            full(8, 4, 256, 128),
            full(2, 128, 512),
            half(32, 512),
            half(32, 512),
            half(2, 16, 32, 512),
            half(1024, 512),
            half(1024, 512),
            half(4, 32, 512),
            half(128, 512),
            full(128, 128),
            half(4, 32, 512),
            full(4, 32, 128),
            full(2, 16, 8, 512),
            pltpu.SMEM((8,), F32),
            pltpu.SMEM((8,), F32),
            dma((N_COPIES,)),
            dma((N_COPIES,)),
            dma((11,)),
            dma((5,)),
        ],
        compiler_params=pltpu.CompilerParams(
            collective_id=0, has_side_effects=True, vmem_limit_bytes=62 * 2**20
        ),
    )(
        tokens, pore_mask, solid_embed.reshape(1, 512), fine_query, fine_key, fine_value, fine_out,
        coarse_query, coarse_key, coarse_value, coarse_out, mlp_in, mlp_out,
        block_ones(), query_table(), key_tables(), fine_scale, coarse_scale,
    )


def solution(mesh):
    placed = (P("tile", "region", None), P("tile", "region")) + (P(),) * 13
    return jax.shard_map(
        body, mesh=mesh, in_specs=placed, out_specs=P("tile", "region", None), check_vma=False
    )
```
